256 devices in a mesh: grp: 16 (over z_hi, y, core), seq: 4 (over z_lo), head: 4 (over x).
Axes of the slice: x: 4, y: 4, z: 8 (z_hi: 2, z_lo: 4; z = z_hi * 4 + z_lo), core: 2. Of those that a mesh axis runs over, the one named last changes fastest.
Arguments:
- t_query: bfloat16 [16, 1024, 2048], P('grp', 'seq', 'head'), may hold values from -8 to 8
- t_key: bfloat16 [16, 1024, 2048], P('grp', 'seq', 'head'), may hold values from -4 to 4
- t_value: bfloat16 [16, 1024, 2048], P('grp', 'seq', 'head'), may hold values from -6 to 6
- out_proj: bfloat16 [2048, 4096], P('head', 'seq'), may hold values from -0.125 to 0.125
- depth_in: bfloat16 [2, 4096, 1024], P(None, 'seq'), may hold values from -0.09375 to 0.09375
- prev_embed: bfloat16 [16, 4, 256, 2, 1024], P('grp', 'head', 'seq'), may hold values from -3 to 3
- cotangent: bfloat16 [16, 4, 256, 2, 1024], P('grp', 'head', 'seq'), may hold values from -0.59765625 to 0.59765625
Outputs:
- d_query: float32 [16, 1024, 2048], P('grp', 'seq', 'head')
- d_key: float32 [16, 1024, 2048], P('grp', 'seq', 'head')
- d_value: float32 [16, 1024, 2048], P('grp', 'seq', 'head')
- d_out_proj: float32 [2048, 4096], P('head', 'seq')
- d_depth_in: float32 [2, 4096, 1024], P(None, ('seq', 'head'), 'grp')
The draws below stay inside these ranges and needn't reach their ends.
All inputs are finite; a program needn't handle non-finite values.
Results may differ from the reference program's by a relative error of at most 0.023.
Values may be sent and summed in bfloat16 or wider, within the bound.
A program may use at most 128 MiB of HBM per device.

```python
import jax
import jax.numpy as jnp
from jax import lax

D = 4096
HT = 16
HD = 128
DD = 1024
KS = 2
LEN = 1024
SEQS = 16
N_HEAD = 4


def draw_t_query(key, part):
    key = jax.random.fold_in(key, 11)
    shape = (SEQS, LEN, HT, HD)
    drawn = jnp.clip(jax.random.normal(key, shape, jnp.float32), -4.0, 4.0)
    return drawn.reshape(SEQS, LEN, HT * HD).astype(jnp.bfloat16)


def draw_t_key(key, part):
    key = jax.random.fold_in(key, 13)
    shape = (SEQS, LEN, HT, HD)
    drawn = jnp.clip(jax.random.normal(key, shape, jnp.float32), -4.0, 4.0)
    return drawn.reshape(SEQS, LEN, HT * HD).astype(jnp.bfloat16)


def draw_prev_embed(key, part):
    key = jax.random.fold_in(key, 23)
    key_base, key_rows, key_cols = jax.random.split(key, 3)
    shape = (SEQS, LEN, KS, DD)
    col_scale = 10.0 ** jax.random.uniform(key_cols, (1, 1, KS, DD), jnp.float32, 0.0, 1.0)
    row_scale = 10.0 ** jax.random.uniform(key_rows, (SEQS, LEN, KS, 1), jnp.float32, -0.5, 0.5)
    base_draw = jnp.clip(jax.random.normal(key_base, shape, jnp.float32), -4.0, 4.0)
    drawn = jnp.clip(0.015 * base_draw * row_scale * col_scale, -3.0, 3.0)
    return drawn.reshape(SEQS, N_HEAD, LEN // N_HEAD, KS, DD).astype(jnp.bfloat16)


def raised(entries, stream_key, source, target, parts, factor):
    owner, partner = [(jnp.arange(entries.shape[axis_at]) // (entries.shape[axis_at] // parts)).reshape([-1 if axis == axis_at else 1 for axis in range(entries.ndim)]) for axis_at in (source, target)]
    chosen = jax.random.permutation(stream_key, parts)[partner]
    strong = (owner == chosen) | (owner == (partner + parts // 2) % parts)
    return jnp.where(strong, factor * entries, entries)


def steps_of(stream_key, shape, cuts, least, largest):
    loudness, own = 1.0, jax.random.fold_in(stream_key, 6)
    for position, parts in cuts:
        draws = jnp.exp(jax.random.uniform(jax.random.fold_in(own, position), (parts,), jnp.float32, least / len(cuts), largest / len(cuts)))
        loudness = loudness * jnp.repeat(draws, shape[position] // parts).reshape([-1 if axis == position else 1 for axis in range(len(shape))])
    return loudness


def centred(own_key, shape, spread, reach, shards=(), held_as=jnp.bfloat16):
    loudness = steps_of(own_key, shape, shards, -0.22, 0.18) if shards else 1.0
    values = jax.random.normal(own_key, shape, jnp.float32) * spread * loudness
    return jnp.minimum(jnp.maximum(values, -reach), reach).astype(held_as)


def noise_with(stream_key, dims, spread, bound, cuts, heavy, kind=jnp.bfloat16):
    result = spread * jax.random.normal(stream_key, dims, jnp.float32)
    if cuts:
        result = result * steps_of(stream_key, dims, cuts, -0.22, 0.18)
    return jnp.clip(raised(result, jax.random.fold_in(stream_key, 3), *heavy), -bound, bound).astype(kind)


def setup_inputs(seed: int = 0) -> dict:
    streams_of = jax.random.split(jax.random.key(seed), 8)
    t_query = draw_t_query(jax.random.fold_in(streams_of[7], 71), 0)
    t_key = draw_t_key(jax.random.fold_in(streams_of[7], 71), 0)
    t_value = centred(streams_of[2], (SEQS, LEN, HT * HD), 1.0, 6.0, ((0, 16), (1, 4), (2, 4)))
    out_proj = centred(streams_of[3], (HT * HD, D), (HT * HD) ** -0.5, 0.125, ((0, 4), (1, 4)))
    depth_in = centred(streams_of[4], (KS, D, DD), D ** -0.5, 0.09375, ((1, 4),))
    prev_embed = draw_prev_embed(jax.random.fold_in(streams_of[7], 71), 0)
    cotangent = noise_with(streams_of[6], (SEQS, N_HEAD, LEN // N_HEAD, KS, DD), 0.1, 0.59765625, ((0, 16), (1, 4), (2, 4)), (0, 4, 16, 2.0))
    return {"t_query": t_query, "t_key": t_key, "t_value": t_value, "out_proj": out_proj, "depth_in": depth_in, "prev_embed": prev_embed, "cotangent": cotangent}


def attention_forward(query_rows, key_rows, value_rows):
    score_scale = HD ** (-0.5)
    query_heads = query_rows.reshape(LEN, HT, HD).astype(jnp.float32)
    key_heads = key_rows.reshape(LEN, HT, HD).astype(jnp.float32)
    value_heads = value_rows.reshape(LEN, HT, HD).astype(jnp.float32)
    scores = jnp.einsum('qhd,khd->hqk', query_heads, key_heads) * score_scale
    positions = jnp.arange(LEN, dtype=jnp.int32)
    causal = positions[:, None] >= positions[None, :]
    scores = jnp.where(causal, scores, -1e+30)
    row_max = lax.optimization_barrier(jnp.max(scores, axis=-1, keepdims=True))
    expo_terms = jnp.where(causal, jnp.exp(scores - row_max), 0.0)
    row_total = lax.optimization_barrier(jnp.sum(expo_terms, axis=-1))
    rounded = lax.optimization_barrier(expo_terms.astype(jnp.bfloat16)).astype(jnp.float32)
    mixed_heads = jnp.einsum('hqk,khd->qhd', rounded, value_heads) / jnp.transpose(row_total)[:, :, None]
    attended = mixed_heads.reshape(LEN, HT * HD).astype(jnp.bfloat16)
    return (attended, expo_terms / row_total[:, :, None])

def attention_backward(query_rows, key_rows, value_rows, attended, probability, grad_attended):
    score_scale = HD ** (-0.5)
    query_heads = query_rows.reshape(LEN, HT, HD).astype(jnp.float32)
    key_heads = key_rows.reshape(LEN, HT, HD).astype(jnp.float32)
    value_heads = value_rows.reshape(LEN, HT, HD).astype(jnp.float32)
    grad_heads = grad_attended.reshape(LEN, HT, HD).astype(jnp.float32)
    attended_heads = attended.reshape(LEN, HT, HD).astype(jnp.float32)
    grad_probs = jnp.einsum('qhd,khd->hqk', grad_heads, value_heads)
    delta_rows = jnp.transpose(lax.optimization_barrier(jnp.sum(grad_heads * attended_heads, axis=-1)))
    grad_scores = probability * (grad_probs - delta_rows[:, :, None])
    grad_scores = lax.optimization_barrier(grad_scores.astype(jnp.bfloat16)).astype(jnp.float32)
    prob_rounded = lax.optimization_barrier(probability.astype(jnp.bfloat16)).astype(jnp.float32)
    grad_query = jnp.einsum('hqk,khd->qhd', grad_scores, key_heads) * score_scale
    grad_key = jnp.einsum('hqk,qhd->khd', grad_scores, query_heads) * score_scale
    grad_value = jnp.einsum('hqk,qhd->khd', prob_rounded, grad_heads)
    return (grad_query.reshape(LEN, HT * HD), grad_key.reshape(LEN, HT * HD), grad_value.reshape(LEN, HT * HD))

def reference(t_query, t_key, t_value, out_proj, depth_in, prev_embed, cotangent):
    wide_in = depth_in.astype(jnp.float32)

    def one_sequence(partial_sums, seq_items):
        query_rows, key_rows, value_rows, embed_rows, grad_rows = seq_items
        attended, probability = attention_forward(query_rows, key_rows, value_rows)
        context = jnp.dot(attended, out_proj, preferred_element_type=jnp.float32).astype(jnp.bfloat16)
        context_wide = context.astype(jnp.float32)
        depth_x = jnp.einsum('fd,kdc->fkc', context_wide, wide_in)
        depth_x = depth_x + embed_rows.reshape(LEN, KS, DD).astype(jnp.float32)
        inverse = lax.rsqrt(lax.optimization_barrier(jnp.mean(depth_x * depth_x, axis=-1, keepdims=True)) + 1e-05)
        normed = depth_x * inverse
        grad_out = grad_rows.reshape(LEN, KS, DD).astype(jnp.float32)
        grad_x = inverse * (grad_out - normed * lax.optimization_barrier(jnp.mean(grad_out * normed, axis=-1, keepdims=True)))
        grad_x = lax.optimization_barrier(grad_x.astype(jnp.bfloat16)).astype(jnp.float32)
        grad_win = jnp.einsum('fd,fkc->kdc', context_wide, grad_x)
        grad_context = jnp.einsum('fkc,kdc->fd', grad_x, wide_in).astype(jnp.bfloat16)
        grad_wo = jnp.dot(jnp.transpose(attended), grad_context, preferred_element_type=jnp.float32)
        grad_attended = jnp.dot(grad_context, jnp.transpose(out_proj), preferred_element_type=jnp.float32).astype(jnp.bfloat16)
        grads = attention_backward(query_rows, key_rows, value_rows, attended, probability, grad_attended)
        return ((partial_sums[0] + grad_wo, partial_sums[1] + grad_win), grads)
    zero_init = (jnp.zeros((HT * HD, D), jnp.float32), jnp.zeros((KS, D, DD), jnp.float32))
    sums, grads = lax.scan(one_sequence, zero_init, (t_query, t_key, t_value, prev_embed, cotangent))
    return (grads[0], grads[1], grads[2], sums[0], sums[1])
```

```python
import jax
import jax.numpy as jnp
from jax import lax
from jax.experimental import pallas as pl
from jax.experimental.pallas import tpu as pltpu
from jax.sharding import PartitionSpec as P

MESH = pl.DeviceIdType.MESH
HD = 128
BF = jnp.bfloat16
F32 = jnp.float32
SCALE = HD ** (-0.5)
LOG2E = 1.4426950408889634


def nt(a, b):
    return lax.dot_general(a, b, (((1,), (1,)), ((), ())), preferred_element_type=F32)


def nn(a, b):
    return jnp.dot(a, b, preferred_element_type=F32)


def transposed(a):
    return jnp.transpose(a.astype(F32)).astype(BF)


def kernel(
    q, k, v, wo, di, pe, ct,
    dq, dk, dv, dw, dd,
    q_all, k_all, v_all, w_v, d_v, pe_v, ct_v,
    m_part, m_recv, m_own, m_all,
    vt, kt, p_t, a_loc, a_r, af, aft,
    xp, xr, gx_all, ga_f, ga_h,
    dk_acc, dv_acc, dq_b, dk_b, dv_b,
    g_send, g_own, g_r1, g2, g_r2, g3, g_r3, grow, dop, gperm, gcol, ddp, dd_r, dd_o,
    loc, qkv_s, qkv_r, mr_s, mr_r, ma_s, ma_r, my_s, my_r, mc_s, mc_r,
    a_s, a_rs, x_s, x_r, gx_s, gx_r, ga_s, ga_r, o_s, o_r,
    g1_s, g1_r, g2_s, g2_r, g3_s, g3_r, g4_s, g4_r, gc_s, gc_r, h_s, h_r,
    z_s, z_r, y_s, y_r, c_s, c_r,
):
    g, s, h = lax.axis_index("grp"), lax.axis_index("seq"), lax.axis_index("head")
    zh, y, c = g // 8, (g // 2) % 4, g % 2
    ring = (1, 2, 3)
    seq_at = lambda o: {"seq": (s + o) % 4}
    head_at = lambda o: {"head": (h + o) % 4}
    y_at = lambda o: {"grp": zh * 8 + ((y + o) % 4) * 2 + c}
    core_at = {"grp": zh * 8 + y * 2 + (1 - c)}
    zh_at = {"grp": (1 - zh) * 8 + y * 2 + c}

    def z_at(o):
        other = (zh * 4 + s + o) % 8
        return other // 4, other % 4

    sent = []

    def push(src, dst, send_sem, recv_sem, device):
        copy = pltpu.make_async_remote_copy(
            src_ref=src, dst_ref=dst, send_sem=send_sem, recv_sem=recv_sem,
            device_id=device, device_id_type=MESH,
        )
        copy.start()
        sent.append(copy)
        return copy

    def cols(index):
        return pl.ds(pl.multiple_of(index * HD, HD), HD)

    loads = [
        (wo, w_v), (di, d_v), (pe.at[0, 0], pe_v), (ct.at[0, 0], ct_v),
        (q.at[0, :, cols(s)], q_all.at[s]), (k.at[0, :, cols(s)], k_all.at[s]),
        (v.at[0, :, cols(s)], v_all.at[s]),
    ]
    loads = [pltpu.make_async_copy(src, dst, loc.at[i]) for i, (src, dst) in enumerate(loads)]
    for copy in loads:
        copy.start()

    barrier = pltpu.get_barrier_semaphore()
    greet = lambda device: pl.semaphore_signal(barrier, inc=1, device_id=device, device_id_type=MESH)
    for o in ring:
        greet(seq_at(o))
        greet(head_at(o))
        greet({"grp": (1 - zh) * 8 + y * 2 + c, "seq": (s + o) % 4})
    for o in range(1, 16):
        greet({"grp": (g + o) % 16})

    loads[0].wait()
    loads[1].wait()
    row0 = pl.multiple_of((c * 4 + y) * 64, 64)
    w_rows = w_v[pl.ds(row0, 64), :]
    for step in range(2):
        part = nn(w_rows, d_v[step])
        for half in range(2):
            m_part[2 * step + half] = part[:, half * 512 : half * 512 + 512].astype(BF)
    pl.semaphore_wait(barrier, 24)

    m_rs = [
        push(m_part.at[(s + o) % 4], m_recv.at[o - 1], mr_s.at[o - 1], mr_r.at[o - 1], seq_at(o))
        for o in ring
    ]
    qkv = []
    for n, (src, dst) in enumerate(((k, k_all), (q, q_all), (v, v_all))):
        for o in ring:
            qkv.append(
                push(
                    src.at[0, :, cols((s + o) % 4)], dst.at[s],
                    qkv_s.at[n * 3 + o - 1], qkv_r.at[n * 3 + o - 1], seq_at(o),
                )
            )

    for copy in m_rs:
        copy.wait_recv()
    total = m_part[s].astype(F32)
    for o in ring:
        total += m_recv[o - 1].astype(F32)
    m_own[...] = total.astype(BF)
    m_all[s, pl.ds(row0, 64), :] = m_own[...]
    m_ag = [
        push(m_own, m_all.at[s, pl.ds(row0, 64), :], ma_s.at[o - 1], ma_r.at[o - 1], seq_at(o))
        for o in ring
    ]
    for copy in m_ag:
        copy.wait_recv()
    rows = m_all.at[:, pl.ds(row0, 64), :]
    m_ys = [push(rows, rows, my_s.at[o - 1], my_r.at[o - 1], y_at(o)) for o in ring]

    for copy in loads[2:]:
        copy.wait()
    for copy in qkv:
        copy.wait_recv()
    for i in range(4):
        vt[:, i * 256 : i * 256 + 256] = transposed(v_all[i])
        kt[:, i * 256 : i * 256 + 256] = transposed(k_all[i])
    visible = lax.broadcasted_iota(jnp.int32, (256, 256), 0) <= lax.broadcasted_iota(
        jnp.int32, (256, 256), 1
    )
    a_cp = []
    for i in range(4):
        kk = (i + 1) * 256
        st = nt(k_all[0 : i + 1].reshape(kk, HD), q_all[i])
        diagonal = jnp.where(visible, st[i * 256 :], -1e30)
        st = diagonal if i == 0 else jnp.concatenate([st[: i * 256], diagonal], axis=0)
        top = jnp.max(st, axis=0, keepdims=True)
        e = jnp.exp2((st - top) * (SCALE * LOG2E))
        inverse = 1.0 / jnp.sum(e, axis=0, keepdims=True)
        p = (e * inverse).astype(BF)
        p_t[i, 0:kk] = p
        a_loc[i] = jnp.transpose(nn(vt[:, 0:kk], p)).astype(BF).reshape(4, 64, HD)
        a_r[i, s] = a_loc[i, s]
        for o in ring:
            at = i * 3 + o - 1
            a_cp.append(
                push(a_loc.at[i, (s + o) % 4], a_r.at[i, s], a_s.at[at], a_rs.at[at], seq_at(o))
            )

    for copy in m_ys:
        copy.wait_recv()
    half = m_all.at[:, pl.ds(pl.multiple_of(c * 256, 256), 256), :]
    m_c = push(half, half, mc_s, mc_r, core_at)

    for copy in a_cp:
        copy.wait_recv()
    for i in range(4):
        for src in range(4):
            af[i * 64 : i * 64 + 64, src * HD : src * HD + HD] = a_r[i, src]
    m_c.wait_recv()

    for t in range(4):
        xp[:, :, t * 512 : t * 512 + 512] = nn(af[...], m_all[t]).astype(BF).reshape(4, 64, 512)
    x_cp = [
        push(xp.at[(h + o) % 4], xr.at[o - 1], x_s.at[o - 1], x_r.at[o - 1], head_at(o))
        for o in ring
    ]
    for i in range(2):
        aft[i] = transposed(af[:, i * 256 : i * 256 + 256])
    for copy in x_cp:
        copy.wait_recv()
    for step in range(2):
        at = slice(step * 1024, step * 1024 + 1024)
        x = xp[h, :, at].astype(F32)
        for o in ring:
            x += xr[o - 1, :, at].astype(F32)
        x += pe_v[:, at].astype(F32)
        r = lax.rsqrt(jnp.mean(x * x, axis=-1, keepdims=True) + 1e-05)
        normed = x * r
        co = ct_v[:, at].astype(F32)
        gx = r * (co - normed * jnp.mean(co * normed, axis=-1, keepdims=True))
        gx_all[h, :, at] = gx.astype(BF)
    gx_cp = [
        push(gx_all.at[h], gx_all.at[h], gx_s.at[o - 1], gx_r.at[o - 1], head_at(o)) for o in ring
    ]
    for copy in gx_cp:
        copy.wait_recv()

    ga = jnp.zeros((256, 512), F32)
    for t in range(4):
        ga += nt(gx_all[:, :, t * 512 : t * 512 + 512].reshape(256, 512), m_all[t])
    for src in range(4):
        ga_f[src] = ga[:, src * HD : src * HD + HD].astype(BF).reshape(4, 64, HD)
    ga_h[:, s] = ga_f[s]
    ga_cp = [
        push(ga_f.at[(s + o) % 4], ga_h.at[:, s], ga_s.at[o - 1], ga_r.at[o - 1], seq_at(o))
        for o in ring
    ]
    for t in range(4):
        at = slice(t * 512, t * 512 + 512)
        g_send[:, at] = nn(aft[1 - c], gx_all[:, :, at].reshape(256, 512)).astype(BF)
    g1 = push(g_send, g_r1, g1_s, g1_r, core_at)
    for t in range(4):
        at = slice(t * 512, t * 512 + 512)
        g_own[:, at] = nn(aft[c], gx_all[:, :, at].reshape(256, 512))

    for copy in ga_cp:
        copy.wait_recv()

    out_cp = []

    def backward(i):
        kk = (i + 1) * 256
        ga_i = ga_h[i].reshape(256, HD)
        dpt = nt(v_all[0 : i + 1].reshape(kk, HD), ga_i)
        a_i = a_loc[i].reshape(256, HD)
        delta = jnp.sum(jnp.transpose(ga_i.astype(F32) * a_i.astype(F32)), axis=0, keepdims=True)
        p = p_t[i, 0:kk]
        ds = (p.astype(F32) * (dpt - delta)).astype(BF)
        dv_i, dk_i = nn(p, ga_i), nn(ds, q_all[i])
        if i == 3:
            dv_acc[...] = dv_i
            dk_acc[...] = dk_i
        else:
            dv_acc[0:kk] += dv_i
            dk_acc[0:kk] += dk_i
        dq_b[i] = (jnp.transpose(nn(kt[:, 0:kk], ds)) * SCALE).astype(BF)
        dk_b[i] = (dk_acc[i * 256 : kk] * SCALE).astype(BF)
        dv_b[i] = dv_acc[i * 256 : kk].astype(BF)

        outs = ((dq_b, dq), (dk_b, dk), (dv_b, dv))
        o = (i - s + 4) % 4
        remote, local = [], []
        for n, (src, dst) in enumerate(outs):
            remote.append(
                pltpu.make_async_remote_copy(
                    src_ref=src.at[i], dst_ref=dst.at[0, :, cols(s)],
                    send_sem=o_s.at[n * 4 + i], recv_sem=o_r.at[n * 4 + o],
                    device_id={"seq": i}, device_id_type=MESH,
                )
            )
            local.append(
                pltpu.make_async_copy(src.at[i], dst.at[0, :, cols(s)], o_s.at[n * 4 + i])
            )

        @pl.when(s != i)
        def _():
            for copy in remote:
                copy.start()

        @pl.when(s == i)
        def _():
            for copy in local:
                copy.start()

        out_cp.append((i, remote, local))

    backward(3)
    g1.wait_recv()
    g2[...] = (g_own[...] + g_r1[...].astype(F32)).astype(BF).reshape(4, 64, 2048)
    g2c = [
        push(g2.at[(y + o) % 4], g_r2.at[o - 1], g2_s.at[o - 1], g2_r.at[o - 1], y_at(o))
        for o in ring
    ]
    backward(2)
    backward(1)
    backward(0)

    for copy in g2c:
        copy.wait_recv()
    total = g2[y].astype(F32)
    for o in ring:
        total += g_r2[o - 1].astype(F32)
    for t in range(4):
        g3[:, t] = total[:, t * 512 : t * 512 + 512].astype(BF).reshape(2, 32, 512)
    g3c = []
    for o in range(1, 8):
        oz, os = z_at(o)
        g3c.append(
            push(
                g3.at[oz, os], g_r3.at[o - 1], g3_s.at[o - 1], g3_r.at[o - 1],
                {"grp": oz * 8 + y * 2 + c, "seq": os},
            )
        )
    for copy in g3c:
        copy.wait_recv()
    total = g3[zh, s].astype(F32)
    for o in range(1, 8):
        total += g_r3[o - 1].astype(F32)
    grow[s] = total.astype(BF)
    g4c = [push(grow.at[s], grow.at[s], g4_s.at[o - 1], g4_r.at[o - 1], seq_at(o)) for o in ring]
    for copy in g4c:
        copy.wait_recv()

    block = c * 8 + y * 2 + zh
    for j in range(16):
        t, at = j // 8, (j % 8) * 64
        gperm[j] = jnp.concatenate([grow[t, :, at : at + 64], grow[2 + t, :, at : at + 64]], axis=1)
    gcol[block] = gperm[g]
    gcc = [
        push(
            gperm.at[(g + o) % 16], gcol.at[block], gc_s.at[o - 1], gc_r.at[o - 1],
            {"grp": (g + o) % 16},
        )
        for o in range(1, 16)
    ]
    mine = jnp.zeros((32, 1024), F32)
    for t in range(4):
        mine += nt(grow[t], d_v[t // 2, :, (t % 2) * 512 : (t % 2) * 512 + 512])
    out_rows = dop.at[pl.ds(pl.multiple_of(block * 32, 32), 32)]
    out_rows[...] = mine.astype(BF)
    z1 = push(out_rows, out_rows, z_s, z_r, zh_at)

    for copy in gcc:
        copy.wait_recv()
    gct = transposed(gcol[...].reshape(512, HD))
    for j in range(4):
        ddp[j] = nn(gct, w_v[:, j * 256 : j * 256 + 256]).astype(BF)
    hc = [
        push(ddp.at[(h + o) % 4], dd_r.at[o - 1], h_s.at[o - 1], h_r.at[o - 1], head_at(o))
        for o in ring
    ]

    z1.wait_recv()
    rows = dop.at[pl.ds(pl.multiple_of((c * 4 + y) * 64, 64), 64)]
    y1 = [push(rows, rows, y_s.at[o - 1], y_r.at[o - 1], y_at(o)) for o in ring]
    for copy in hc:
        copy.wait_recv()
    total = ddp[h].astype(F32)
    for o in ring:
        total += dd_r[o - 1].astype(F32)
    dd_o[...] = jnp.transpose(total)
    dd_c = pltpu.make_async_copy(dd_o, dd, loc.at[7])
    dd_c.start()
    for copy in y1:
        copy.wait_recv()
    core_rows = pl.ds(pl.multiple_of(c * 256, 256), 256)
    c1 = push(dop.at[core_rows], dw.at[core_rows], c_s, c_r, core_at)
    dw_c = pltpu.make_async_copy(dop.at[core_rows], dw.at[core_rows], loc.at[8])
    dw_c.start()

    for i, remote, local in out_cp:

        @pl.when(s != i)
        def _():
            for copy in remote:
                copy.wait_send()

        @pl.when(s == i)
        def _():
            for copy in local:
                copy.wait()

    for n, (src, dst) in enumerate(((dq_b, dq), (dk_b, dk), (dv_b, dv))):
        for o in ring:
            pltpu.make_async_remote_copy(
                src_ref=src.at[0], dst_ref=dst.at[0, :, cols(s)],
                send_sem=o_s.at[n * 4], recv_sem=o_r.at[n * 4 + o],
                device_id=seq_at(o), device_id_type=MESH,
            ).wait_recv()
    c1.wait_recv()
    dw_c.wait()
    dd_c.wait()
    for copy in sent:
        copy.wait_send()


def shards(t_query, t_key, t_value, out_proj, depth_in, prev_embed, cotangent):
    prev = prev_embed.reshape(1, 1, 64, 2048)
    cot = cotangent.reshape(1, 1, 64, 2048)
    vmem = lambda shape, kind=BF: pltpu.VMEM(shape, kind)
    dma = lambda *n: pltpu.SemaphoreType.DMA(n)
    frames = jax.ShapeDtypeStruct((1, 256, 512), BF)
    dq, dk, dv, dw, dd = pl.pallas_call(
        kernel,
        out_shape=(
            frames, frames, frames,
            jax.ShapeDtypeStruct((512, 1024), BF), jax.ShapeDtypeStruct((256, 128), F32),
        ),
        in_specs=[pl.BlockSpec(memory_space=pl.ANY)] * 7,
        out_specs=[pl.BlockSpec(memory_space=pl.ANY)] * 5,
        scratch_shapes=[
            vmem((4, 256, HD)), vmem((4, 256, HD)), vmem((4, 256, HD)),
            vmem((512, 1024)), vmem((2, 1024, 1024)), vmem((64, 2048)), vmem((64, 2048)),
            vmem((4, 64, 512)), vmem((3, 64, 512)), vmem((64, 512)), vmem((4, 512, 512)),
            vmem((HD, 1024)), vmem((HD, 1024)), vmem((4, 1024, 256)),
            vmem((4, 4, 64, HD)), vmem((4, 4, 64, HD)), vmem((256, 512)), vmem((2, 256, 256)),
            vmem((4, 64, 2048)), vmem((3, 64, 2048)), vmem((4, 64, 2048)),
            vmem((4, 4, 64, HD)), vmem((4, 4, 64, HD)),
            vmem((1024, HD), F32), vmem((1024, HD), F32),
            vmem((4, 256, HD)), vmem((4, 256, HD)), vmem((4, 256, HD)),
            vmem((256, 2048)), vmem((256, 2048), F32), vmem((256, 2048)),
            vmem((4, 64, 2048)), vmem((3, 64, 2048)), vmem((2, 4, 32, 512)), vmem((7, 32, 512)),
            vmem((4, 32, 512)), vmem((512, 1024)), vmem((16, 32, HD)), vmem((16, 32, HD)),
            vmem((4, HD, 256)), vmem((3, HD, 256)), vmem((256, HD), F32),
            dma(9), dma(9), dma(9), dma(3), dma(3), dma(3), dma(3), dma(3), dma(3), dma(), dma(),
            dma(12), dma(12), dma(3), dma(3), dma(3), dma(3), dma(3), dma(3), dma(12), dma(12),
            dma(), dma(), dma(3), dma(3), dma(7), dma(7), dma(3), dma(3), dma(15), dma(15),
            dma(3), dma(3), dma(), dma(), dma(3), dma(3), dma(), dma(),
        ],
        compiler_params=pltpu.CompilerParams(
            collective_id=0, has_side_effects=True, vmem_limit_bytes=48 * 1024 * 1024
        ),
    )(t_query, t_key, t_value, out_proj, depth_in, prev, cot)
    grad_depth = jnp.transpose(dd.reshape(256, 2, 64), (1, 0, 2))
    return dq.astype(F32), dk.astype(F32), dv.astype(F32), dw.astype(F32), grad_depth


def solution(mesh):
    placed = (
        P("grp", "seq", "head"),
        P("grp", "seq", "head"),
        P("grp", "seq", "head"),
        P("head", "seq"),
        P(None, "seq", None),
        P("grp", "head", "seq", None, None),
        P("grp", "head", "seq", None, None),
    )
    return jax.shard_map(
        shards,
        mesh=mesh,
        in_specs=placed,
        out_specs=(
            P("grp", "seq", "head"),
            P("grp", "seq", "head"),
            P("grp", "seq", "head"),
            P("head", "seq"),
            P(None, ("seq", "head"), "grp"),
        ),
        check_vma=False,
    )
```

```python
import jax
import jax.numpy as jnp
from jax import lax
from jax.experimental import pallas as pl
from jax.experimental.pallas import tpu as pltpu
from jax.sharding import PartitionSpec as P

MESH = pl.DeviceIdType.MESH
HD = 128
BF = jnp.bfloat16
F32 = jnp.float32
SCALE = HD ** (-0.5)
LOG2E = 1.4426950408889634


def nt(a, b):
    return lax.dot_general(a, b, (((1,), (1,)), ((), ())), preferred_element_type=F32)


def nn(a, b):
    return jnp.dot(a, b, preferred_element_type=F32)


def transposed(a):
    return jnp.transpose(a.astype(F32)).astype(BF)


def kernel(
    q, k, v, wo, di, pe, ct,
    dq, dk, dv, dw, dd,
    q_all, k_all, v_all, w_v, d_v, pe_v, ct_v, pe_w, ct_w,
    m_part, m_recv, m_own, m_all,
    vt, kt, p_t, a_loc, a_r, af, aft,
    xp, x_land, gx_all, ga_f, ga_h,
    dk_acc, dv_acc, dq_b, dk_b, dv_b,
    g_send, g_r1, g2, g_land, g3, g_r3, grow, dop, gperm, gcol, ddp, dd_r, dd_o,
    loc, qkv_s, qkv_r, mr_s, mr_r, ma_s, ma_r, my_s, my_r, mc_s, mc_r,
    a_s, a_rs, x_s, x_r, gx_s, gx_r, ga_s, ga_r, o_s, o_r,
    g1_s, g1_r, g2_s, g2_r, g3_s, g3_r, g4_s, g4_r, gc_s, gc_r, h_s, h_r,
    y_s, y_r, c_s, c_r,
):
    g, s, h = lax.axis_index("grp"), lax.axis_index("seq"), lax.axis_index("head")
    zh, y, c = g // 8, (g // 2) % 4, g % 2
    ring = (1, 2, 3)
    seq_at = lambda o: {"seq": (s + o) % 4}
    head_at = lambda o: {"head": (h + o) % 4}
    y_at = lambda o: {"grp": zh * 8 + ((y + o) % 4) * 2 + c}
    core_at = {"grp": zh * 8 + y * 2 + (1 - c)}

    half_at = lambda o: {"grp": zh * 8 + (g + o) % 8}

    def z_at(o):
        other = (zh * 4 + s + o) % 8
        return other // 4, other % 4

    def z_device(o):
        oz, os = z_at(o)
        return {"grp": oz * 8 + y * 2 + c, "seq": os}

    sent = []

    def push(src, dst, send_sem, recv_sem, device):
        copy = pltpu.make_async_remote_copy(
            src_ref=src, dst_ref=dst, send_sem=send_sem, recv_sem=recv_sem,
            device_id=device, device_id_type=MESH,
        )
        copy.start()
        sent.append(copy)
        return copy

    def ring_sum(part, land, at, i, send, recv):
        right, left = (i + 1) % 4, (i + 3) % 4
        copies = {}

        def go(n, j, half, device):
            copies[n] = push(part.at[j, half], land.at[n], send.at[n], recv.at[n], device)

        def opposite():
            go(0, (i + 2) % 4, 0, at(1))
            go(1, (i + 2) % 4, 1, at(3))

        def to_left():
            go(2, left, 0, at(3))

        def to_right():
            go(3, right, 1, at(1))

        def relay():
            copies[0].wait_recv()
            part[right, 0] = (part[right, 0].astype(F32) + land[0].astype(F32)).astype(BF)
            go(4, right, 0, at(1))
            copies[1].wait_recv()
            part[left, 1] = (part[left, 1].astype(F32) + land[1].astype(F32)).astype(BF)
            go(5, left, 1, at(3))

        def result(half):
            copies[2 + half].wait_recv()
            copies[4 + half].wait_recv()
            total = part[i, half].astype(F32) + land[2 + half].astype(F32)
            return total + land[4 + half].astype(F32)

        return opposite, to_left, to_right, relay, result

    def ring_gather(view, at, i, send, recv):
        copies = {}

        def go(n, j, half, device):
            copies[n] = push(view(j, half), view(j, half), send.at[n], recv.at[n], device)

        def start(half):
            go(2 * half, i, half, at(1))
            go(2 * half + 1, i, half, at(3))

        def relay():
            copies[0].wait_recv()
            go(4, (i + 3) % 4, 0, at(1))
            copies[3].wait_recv()
            go(5, (i + 1) % 4, 1, at(3))

        return start, relay, copies

    def cols(index):
        return pl.ds(pl.multiple_of(index * HD, HD), HD)

    loads = [
        (wo, w_v), (di, d_v), (pe.at[0, 0], pe_v), (ct.at[0, 0], ct_v),
        (q.at[0, :, cols(s)], q_all.at[s]), (k.at[0, :, cols(s)], k_all.at[s]),
        (v.at[0, :, cols(s)], v_all.at[s]),
    ]
    loads = [pltpu.make_async_copy(src, dst, loc.at[i]) for i, (src, dst) in enumerate(loads)]
    for copy in loads:
        copy.start()

    barrier = pltpu.get_barrier_semaphore()
    greet = lambda device: pl.semaphore_signal(barrier, inc=1, device_id=device, device_id_type=MESH)
    for o in ring:
        greet(seq_at(o))
        greet(head_at(o))
    for o in range(1, 8):
        greet(half_at(o))
    for o in range(4):
        greet({"grp": (g + 8) % 16, "seq": (s + o) % 4})

    loads[0].wait()
    loads[1].wait()
    row0 = pl.multiple_of((c * 4 + y) * 64, 64)
    w_rows = w_v[pl.ds(row0, 64), :]
    for step in range(2):
        part = nn(w_rows, d_v[step])
        for half in range(2):
            m_part[2 * step + half] = part[:, half * 512 : half * 512 + 512].astype(BF)
    pl.semaphore_wait(barrier, 17)

    def m_spread(view, land, send, recv):
        copies = []
        for n, (o, at, rows) in enumerate(
            ((1, 1, (0, 64)), (7, 3, (0, 64)), (2, 2, (0, 32)), (6, 2, (32, 32)))
        ):
            there = land(o, rows)
            copies.append(push(view(at, rows), there, send.at[n], recv.at[n], z_device(o)))
        return copies

    m_rs = m_spread(
        lambda at, rows: m_part.at[(s + at) % 4, pl.ds(*rows)],
        lambda o, rows: m_recv.at[{1: 0, 7: 1, 2: 2, 6: 2}[o], pl.ds(*rows)],
        mr_s, mr_r,
    )
    qkv = []

    def spread(n, src, dst):
        for o in ring:
            at = n * 3 + o - 1
            there = src.at[0, :, cols((s + o) % 4)]
            qkv.append(push(there, dst.at[s], qkv_s.at[at], qkv_r.at[at], seq_at(o)))

    spread(0, k, k_all)
    for copy in m_rs:
        copy.wait_recv()
    total = m_part[s].astype(F32)
    for o in ring:
        total += m_recv[o - 1].astype(F32)
    m_own[...] = total.astype(BF)
    m_all[s, pl.ds(row0, 64), :] = m_own[...]
    m_ag = m_spread(
        lambda at, rows: m_own.at[pl.ds(*rows)],
        lambda o, rows: m_all.at[s, pl.ds(pl.multiple_of(row0 + rows[0], 32), rows[1])],
        ma_s, ma_r,
    )
    spread(1, q, q_all)
    spread(2, v, v_all)
    for copy in m_ag:
        copy.wait_recv()
    def m_rows(index):
        return pl.ds(pl.multiple_of((c * 4 + index) * 64, 64), 64)

    m_start, m_relay, m_y = ring_gather(
        lambda j, half: m_all.at[2 * half : 2 * half + 2, m_rows(j)], y_at, y, my_s, my_r
    )
    m_start(0)
    m_start(1)
    m_c = []

    def m_across(n, index):
        there = m_all.at[:, m_rows(index)]
        m_c.append(push(there, there, mc_s.at[n], mc_r.at[n], core_at))

    m_across(0, y)
    m_relay()

    for copy in loads[2:]:
        copy.wait()
    for copy in qkv[:6]:
        copy.wait_recv()
    for i in range(4):
        kt[:, i * 256 : i * 256 + 256] = transposed(k_all[i])
    visible = lax.broadcasted_iota(jnp.int32, (256, 256), 0) <= lax.broadcasted_iota(
        jnp.int32, (256, 256), 1
    )
    for i in range(4):
        kk = (i + 1) * 256
        st = nt(k_all[0 : i + 1].reshape(kk, HD), q_all[i])
        diagonal = jnp.where(visible, st[i * 256 :], -1e30)
        st = diagonal if i == 0 else jnp.concatenate([st[: i * 256], diagonal], axis=0)
        top = jnp.max(st, axis=0, keepdims=True)
        e = jnp.exp2((st - top) * (SCALE * LOG2E))
        inverse = 1.0 / jnp.sum(e, axis=0, keepdims=True)
        p_t[i, 0:kk] = (e * inverse).astype(BF)
    for copy in qkv[6:]:
        copy.wait_recv()
    for i in range(4):
        vt[:, i * 256 : i * 256 + 256] = transposed(v_all[i])
    for i in range(4):
        kk = (i + 1) * 256
        a_loc[i] = jnp.transpose(nn(vt[:, 0:kk], p_t[i, 0:kk])).astype(BF).reshape(4, 64, HD)
    h_order = [(h + o) % 4 for o in (2, 3, 1, 0)]
    a_cp = []
    for n, a in enumerate(h_order):
        a_r[a, s] = a_loc[a, s]
        for o in ring:
            at = n * 3 + o - 1
            a_cp.append(
                push(a_loc.at[a, (s + o) % 4], a_r.at[a, s], a_s.at[at], a_rs.at[at], seq_at(o))
            )

    m_y[2].wait_recv()
    m_across(1, (y + 3) % 4)
    m_y[1].wait_recv()
    m_across(2, (y + 1) % 4)
    m_y[4].wait_recv()
    m_y[5].wait_recv()
    m_across(3, (y + 2) % 4)
    for copy in m_c:
        copy.wait_recv()

    x_opposite, x_left, x_right, x_relay, x_result = ring_sum(xp, x_land, head_at, h, x_s, x_r)
    for n, send in enumerate((x_opposite, x_left, x_right, None)):
        a = h_order[n]
        for copy in a_cp[3 * n : 3 * n + 3]:
            copy.wait_recv()
        for src in range(4):
            af[a, :, src * HD : src * HD + HD] = a_r[a, src]
        for t in range(4):
            there = slice((t % 2) * 512, (t % 2) * 512 + 512)
            xp[a, t // 2, :, there] = nn(af[a], m_all[t]).astype(BF)
        if send is not None:
            send()
    x_relay()
    for step in range(2):
        pe_w[step] = pe_v[:, step, :].astype(F32)
        ct_w[step] = ct_v[:, step, :].astype(F32)
    for i in range(2):
        at = transposed(af[:, :, i * 256 : i * 256 + 256].reshape(256, 256))
        aft[i] = at.reshape(4, 64, 256)
    gx_start, gx_relay, gx_cp = ring_gather(
        lambda j, half: gx_all.at[j, half], head_at, h, gx_s, gx_r
    )
    for step in range(2):
        x = x_result(step) + pe_w[step]
        r = lax.rsqrt(jnp.mean(x * x, axis=-1, keepdims=True) + 1e-05)
        normed = x * r
        co = ct_w[step]
        gx = r * (co - normed * jnp.mean(co * normed, axis=-1, keepdims=True))
        gx_all[h, step] = gx.astype(BF)
        gx_start(step)

    ga_cp = []

    def grad_rows(n, a):
        ga = jnp.zeros((64, 512), F32)
        for t in range(4):
            there = slice((t % 2) * 512, (t % 2) * 512 + 512)
            ga += nt(gx_all[a, t // 2, :, there], m_all[t])
        for src in range(4):
            ga_f[a, src] = ga[:, src * HD : src * HD + HD].astype(BF)
        ga_h[a, s] = ga_f[a, s]
        for o in ring:
            at = n * 3 + o - 1
            ga_cp.append(
                push(ga_f.at[a, (s + o) % 4], ga_h.at[a, s], ga_s.at[at], ga_r.at[at], seq_at(o))
            )

    grad_rows(0, h)
    gx_relay()
    gx_cp[2].wait_recv()
    grad_rows(1, (h + 3) % 4)
    gx_cp[1].wait_recv()
    grad_rows(2, (h + 1) % 4)
    gx_cp[4].wait_recv()
    gx_cp[5].wait_recv()
    grad_rows(3, (h + 2) % 4)

    y_order = [(y + o) % 4 for o in (2, 3, 1, 0)]

    def g_rows(core, index, step):
        return nn(aft[core, index], gx_all[:, step].reshape(256, 1024))

    g1 = []
    for n, index in enumerate(y_order):
        for step in range(2):
            g_send[index, step] = g_rows(1 - c, index, step).astype(BF)
        g1.append(push(g_send.at[index], g_r1.at[index], g1_s.at[n], g1_r.at[n], core_at))

    g_opposite, g_left, g_right, g_relay, g_result = ring_sum(g2, g_land, y_at, y, g2_s, g2_r)
    for n, send in enumerate((g_opposite, g_left, g_right, None)):
        index = y_order[n]
        own = [g_rows(c, index, step) for step in range(2)]
        g1[n].wait_recv()
        for step in range(2):
            g2[index, step] = (own[step] + g_r1[index, step].astype(F32)).astype(BF)
        if send is not None:
            send()

    for copy in ga_cp:
        copy.wait_recv()

    def backward(i):
        kk = (i + 1) * 256
        ga_i = ga_h[i].reshape(256, HD)
        dpt = nt(v_all[0 : i + 1].reshape(kk, HD), ga_i)
        a_i = a_loc[i].reshape(256, HD)
        delta = jnp.sum(jnp.transpose(ga_i.astype(F32) * a_i.astype(F32)), axis=0, keepdims=True)
        p = p_t[i, 0:kk]
        ds = (p.astype(F32) * (dpt - delta)).astype(BF)
        dv_i, dk_i = nn(p, ga_i), nn(ds, q_all[i])
        if i == 3:
            dv_acc[...] = dv_i
            dk_acc[...] = dk_i
        else:
            dv_acc[0:kk] += dv_i
            dk_acc[0:kk] += dk_i
        dq_b[i] = (jnp.transpose(nn(kt[:, 0:kk], ds)) * SCALE).astype(BF)
        dk_b[i] = (dk_acc[i * 256 : kk] * SCALE).astype(BF)
        dv_b[i] = dv_acc[i * 256 : kk].astype(BF)


    for i in (3, 2, 1, 0):
        backward(i)
    outs = ((dq_b, dq), (dk_b, dk), (dv_b, dv))
    out_cp, out_own = [], []

    def give(n):
        src, dst = outs[n]
        there = dst.at[0, :, cols(s)]
        for o in ring:
            at = n * 3 + o - 1
            out_cp.append(push(src.at[(s + o) % 4], there, o_s.at[at], o_r.at[at], seq_at(o)))
        out_own.append(pltpu.make_async_copy(src.at[s], there, loc.at[16 + n]))
        out_own[-1].start()

    give(0)
    g_relay()
    give(1)
    for step in range(2):
        total = g_result(step)
        for t in range(2):
            there = total[:, t * 512 : t * 512 + 512].astype(BF)
            g3[:, 2 * step + t] = there.reshape(2, 32, 512)
    g3c = []
    for o in range(1, 8):
        oz, os = z_at(o)
        g3c.append(
            push(g3.at[oz, os], g_r3.at[o - 1], g3_s.at[o - 1], g3_r.at[o - 1], z_device(o))
        )
    for copy in g3c:
        copy.wait_recv()
    total = g3[zh, s].astype(F32)
    for o in range(1, 8):
        total += g_r3[o - 1].astype(F32)
    grow[s, zh] = total.astype(BF)
    g4c = [
        push(grow.at[s, zh], grow.at[s, zh], g4_s.at[o - 1], g4_r.at[o - 1], z_device(o))
        for o in range(1, 8)
    ]
    give(2)
    for copy in g4c:
        copy.wait_recv()

    for j in range(8):
        there = slice(j * 64, j * 64 + 64)
        pair = [grow[2 * step + zh, :, :, there].reshape(64, 64) for step in range(2)]
        gperm[j] = jnp.concatenate(pair, axis=1)
    block = c * 4 + y
    gcol[block] = gperm[g % 8]
    gcc = [
        push(
            gperm.at[(g + o) % 8], gcol.at[block], gc_s.at[o - 1], gc_r.at[o - 1], half_at(o)
        )
        for o in range(1, 8)
    ]
    y_cp = []
    for half in range(2):
        mine = jnp.zeros((64, 512), F32)
        for t in range(4):
            depth = d_v[t // 2, half * 512 : half * 512 + 512, (t % 2) * 512 : (t % 2) * 512 + 512]
            mine += nt(grow[t].reshape(64, 512), depth)
        dop[half, m_rows(y)] = mine.astype(BF)
        here = dop.at[half, m_rows(y)]
        for o in ring:
            at = half * 3 + o - 1
            y_cp.append(push(here, here, y_s.at[at], y_r.at[at], y_at(o)))

    c1, dw_c = [], []

    def out_across(n, index):
        for half in range(2):
            at = 2 * n + half
            if n:
                y_cp[half * 3 + n - 1].wait_recv()
            here = dop.at[half, m_rows(index)]
            there = dw.at[m_rows(index), half * 512 : half * 512 + 512]
            dw_c.append(pltpu.make_async_copy(here, there, loc.at[8 + at]))
            dw_c[at].start()
            c1.append(push(here, there, c_s.at[at], c_r.at[at], core_at))

    out_across(0, y)
    for copy in gcc:
        copy.wait_recv()
    gct = transposed(gcol[...].reshape(512, HD))
    for j in range(4):
        ddp[j] = nn(gct, w_v[:, j * 256 : j * 256 + 256]).astype(BF)
    hc = [
        push(ddp.at[(h + o) % 4], dd_r.at[o - 1], h_s.at[o - 1], h_r.at[o - 1], head_at(o))
        for o in ring
    ]
    for o in ring:
        out_across(o, (y + 4 - o) % 4)
    for copy in hc:
        copy.wait_recv()
    total = ddp[h].astype(F32)
    for o in ring:
        total += dd_r[o - 1].astype(F32)
    dd_o[...] = total
    dd_c = pltpu.make_async_copy(dd_o, dd, loc.at[7])
    dd_c.start()
    for copy in out_cp:
        copy.wait_recv()
    for copy in out_own:
        copy.wait()
    for copy in c1:
        copy.wait_recv()
    for copy in dw_c:
        copy.wait()
    dd_c.wait()
    for copy in sent:
        copy.wait_send()


def widen(dq, dk, dv, dw, dd, *refs):
    outs, (narrow, tokens, weight, load, store) = refs[:5], refs[5:]
    parts = [(src.at[0], dst.at[0], tokens.at[n]) for n, (src, dst) in enumerate(zip((dq, dk, dv), outs))]
    for n in range(4):
        rows = slice(n * 128, n * 128 + 128)
        for half in range(2):
            at = (rows, slice(half * 512, half * 512 + 512))
            parts.append((dw.at[at], outs[3].at[at], weight.at[n, half]))
    held = [narrow.at[n] if n < 3 else narrow.at[n, 0:128] for n in range(11)]
    loads = [pltpu.make_async_copy(p[0], held[n], load.at[n]) for n, p in enumerate(parts)]
    stores = [pltpu.make_async_copy(p[2], p[1], store.at[n]) for n, p in enumerate(parts)]
    stores.append(pltpu.make_async_copy(dd, outs[4], store.at[11]))
    stores[11].start()
    for copy in loads:
        copy.start()
    for n, part in enumerate(parts):
        loads[n].wait()
        part[2][...] = held[n][...].astype(F32)
        stores[n].start()
    for copy in stores:
        copy.wait()


def shards(t_query, t_key, t_value, out_proj, depth_in, prev_embed, cotangent):
    vmem = lambda shape, kind=BF: pltpu.VMEM(shape, kind)
    dma = lambda *n: pltpu.SemaphoreType.DMA(n)
    frames = jax.ShapeDtypeStruct((1, 256, 512), BF)
    dq, dk, dv, dw, dd = pl.pallas_call(
        kernel,
        out_shape=(
            frames, frames, frames,
            jax.ShapeDtypeStruct((512, 1024), BF), jax.ShapeDtypeStruct((HD, 256), F32),
        ),
        in_specs=[pl.BlockSpec(memory_space=pl.ANY)] * 7,
        out_specs=[pl.BlockSpec(memory_space=pl.ANY)] * 5,
        scratch_shapes=[
            vmem((4, 256, HD)), vmem((4, 256, HD)), vmem((4, 256, HD)),
            vmem((512, 1024)), vmem((2, 1024, 1024)), vmem((64, 2, 1024)), vmem((64, 2, 1024)),
            vmem((2, 64, 1024), F32), vmem((2, 64, 1024), F32),
            vmem((4, 64, 512)), vmem((3, 64, 512)), vmem((64, 512)), vmem((4, 512, 512)),
            vmem((HD, 1024)), vmem((HD, 1024)), vmem((4, 1024, 256)),
            vmem((4, 4, 64, HD)), vmem((4, 4, 64, HD)), vmem((4, 64, 512)), vmem((2, 4, 64, 256)),
            vmem((4, 2, 64, 1024)), vmem((6, 64, 1024)), vmem((4, 2, 64, 1024)),
            vmem((4, 4, 64, HD)), vmem((4, 4, 64, HD)),
            vmem((1024, HD), F32), vmem((1024, HD), F32),
            vmem((4, 256, HD)), vmem((4, 256, HD)), vmem((4, 256, HD)),
            vmem((4, 2, 64, 1024)), vmem((4, 2, 64, 1024)), vmem((4, 2, 64, 1024)),
            vmem((6, 64, 1024)), vmem((2, 4, 32, 512)), vmem((7, 32, 512)),
            vmem((4, 2, 32, 512)), vmem((2, 512, 512)), vmem((8, 64, HD)), vmem((8, 64, HD)),
            vmem((4, HD, 256)), vmem((3, HD, 256)), vmem((HD, 256), F32),
            dma(19), dma(9), dma(9), dma(4), dma(4), dma(4), dma(4), dma(6), dma(6), dma(4), dma(4),
            dma(12), dma(12), dma(6), dma(6), dma(6), dma(6), dma(12), dma(12), dma(9), dma(9),
            dma(4), dma(4), dma(6), dma(6), dma(7), dma(7), dma(7), dma(7), dma(7), dma(7),
            dma(3), dma(3), dma(6), dma(6), dma(8), dma(8),
        ],
        compiler_params=pltpu.CompilerParams(
            collective_id=0, has_side_effects=True, vmem_limit_bytes=60 * 1024 * 1024
        ),
    )(t_query, t_key, t_value, out_proj, depth_in, prev_embed, cotangent)
    wide = lambda *shape: jax.ShapeDtypeStruct(shape, F32)
    dq, dk, dv, dw, dd = pl.pallas_call(
        widen,
        out_shape=(wide(1, 256, 512), wide(1, 256, 512), wide(1, 256, 512), wide(512, 1024), wide(HD, 256)),
        in_specs=[pl.BlockSpec(memory_space=pl.ANY)] * 5,
        out_specs=[pl.BlockSpec(memory_space=pl.ANY)] * 5,
        scratch_shapes=[
            vmem((11, 256, 512)), vmem((3, 256, 512), F32), vmem((4, 2, 128, 512), F32), dma(11), dma(12),
        ],
        compiler_params=pltpu.CompilerParams(vmem_limit_bytes=60 * 1024 * 1024),
    )(dq, dk, dv, dw, dd)
    return dq, dk, dv, dw, jnp.transpose(dd.reshape(2, 64, 256), (0, 2, 1))


def solution(mesh):
    placed = (
        P("grp", "seq", "head"),
        P("grp", "seq", "head"),
        P("grp", "seq", "head"),
        P("head", "seq"),
        P(None, "seq", None),
        P("grp", "head", "seq", None, None),
        P("grp", "head", "seq", None, None),
    )
    return jax.shard_map(
        shards,
        mesh=mesh,
        in_specs=placed,
        out_specs=(
            P("grp", "seq", "head"),
            P("grp", "seq", "head"),
            P("grp", "seq", "head"),
            P("head", "seq"),
            P(None, ("seq", "head"), "grp"),
        ),
        check_vma=False,
    )
```

```python
import jax
import jax.numpy as jnp
from jax import lax
from jax.experimental import pallas as pl
from jax.experimental.pallas import tpu as pltpu
from jax.sharding import PartitionSpec as P

MESH = pl.DeviceIdType.MESH
HD = 128
BF = jnp.bfloat16
F32 = jnp.float32
SCALE = HD ** (-0.5)
LOG2E = 1.4426950408889634


def nt(a, b):
    return lax.dot_general(a, b, (((1,), (1,)), ((), ())), preferred_element_type=F32)


def nn(a, b):
    return jnp.dot(a, b, preferred_element_type=F32)


def transposed(a):
    return jnp.transpose(a.astype(F32)).astype(BF)


def kernel(
    q, k, v, wo, di, pe, ct,
    dq, dk, dv, dw, dd,
    q_all, k_all, v_all, w_v, d_v, pe_v, ct_v, pe_w, ct_w,
    m_part, m_recv, m_own, m_all,
    vt, kt, p_t, a_loc, a_r, af, aft,
    xp, x_land, gx_all, ga_f, ga_h,
    dk_acc, dv_acc, dq_b, dk_b, dv_b,
    g_send, g_r1, g2, g_land, g3, g_r3, grow, dop, gperm, gcol, ddp, dd_r, dd_o,
    loc, qkv_s, qkv_r, mr_s, mr_r, ma_s, ma_r, my_s, my_r, mc_s, mc_r,
    a_s, a_rs, x_s, x_r, gx_s, gx_r, ga_s, ga_r, o_s, o_r,
    g1_s, g1_r, g2_s, g2_r, g3_s, g3_r, g4_s, g4_r, gc_s, gc_r, h_s, h_r,
    y_s, y_r, c_s, c_r,
):
    g, s, h = lax.axis_index("grp"), lax.axis_index("seq"), lax.axis_index("head")
    zh, y, c = g // 8, (g // 2) % 4, g % 2
    ring = (1, 2, 3)
    seq_at = lambda o: {"seq": (s + o) % 4}
    head_at = lambda o: {"head": (h + o) % 4}
    y_at = lambda o: {"grp": zh * 8 + ((y + o) % 4) * 2 + c}
    core_at = {"grp": zh * 8 + y * 2 + (1 - c)}

    half_at = lambda o: {"grp": zh * 8 + (g + o) % 8}

    def z_at(o):
        other = (zh * 4 + s + o) % 8
        return other // 4, other % 4

    def z_device(o):
        oz, os = z_at(o)
        return {"grp": oz * 8 + y * 2 + c, "seq": os}

    sent = []

    def push(src, dst, send_sem, recv_sem, device):
        copy = pltpu.make_async_remote_copy(
            src_ref=src, dst_ref=dst, send_sem=send_sem, recv_sem=recv_sem,
            device_id=device, device_id_type=MESH,
        )
        copy.start()
        sent.append(copy)
        return copy

    def ring_sum(view, land, at, i, send, recv):
        right, left = (i + 1) % 4, (i + 3) % 4
        copies = {}

        def go(n, j, half, device):
            copies[n] = push(view(j, half), land.at[n], send.at[n], recv.at[n], device)

        def add(n, j, half):
            copies[n].wait_recv()
            here = view(j, half)
            here[...] = (here[...].astype(F32) + land[n].astype(F32)).astype(BF)

        def opposite():
            go(0, (i + 2) % 4, 0, at(1))
            go(1, (i + 2) % 4, 1, at(3))

        def to_left():
            go(2, left, 0, at(3))

        def to_right():
            go(3, right, 1, at(1))

        def relay():
            add(0, right, 0)
            go(4, right, 0, at(1))
            add(1, left, 1)
            go(5, left, 1, at(3))

        def result(half):
            copies[2 + half].wait_recv()
            copies[4 + half].wait_recv()
            total = view(i, half)[...].astype(F32) + land[2 + half].astype(F32)
            return total + land[4 + half].astype(F32)

        return opposite, to_left, to_right, relay, result

    def ring_gather(view, at, i, send, recv):
        copies = {}

        def go(n, j, half, device):
            copies[n] = push(view(j, half), view(j, half), send.at[n], recv.at[n], device)

        def start(half):
            go(2 * half, i, half, at(1))
            go(2 * half + 1, i, half, at(3))

        def relay():
            copies[0].wait_recv()
            go(4, (i + 3) % 4, 0, at(1))
            copies[3].wait_recv()
            go(5, (i + 1) % 4, 1, at(3))

        return start, relay, copies

    def cols(index):
        return pl.ds(pl.multiple_of(index * HD, HD), HD)

    loads = [
        (wo, w_v), (di, d_v), (pe.at[0, 0], pe_v), (ct.at[0, 0], ct_v),
        (q.at[0, :, cols(s)], q_all.at[s]), (k.at[0, :, cols(s)], k_all.at[s]),
        (v.at[0, :, cols(s)], v_all.at[s]),
    ]
    loads = [pltpu.make_async_copy(src, dst, loc.at[i]) for i, (src, dst) in enumerate(loads)]
    for copy in loads:
        copy.start()

    barrier = pltpu.get_barrier_semaphore()
    greet = lambda device: pl.semaphore_signal(barrier, inc=1, device_id=device, device_id_type=MESH)
    for o in ring:
        greet(seq_at(o))
        greet(head_at(o))
    for o in range(1, 8):
        greet(half_at(o))
    for o in range(4):
        greet({"grp": (g + 8) % 16, "seq": (s + o) % 4})

    loads[0].wait()
    loads[1].wait()
    row0 = pl.multiple_of((c * 4 + y) * 64, 64)
    w_rows = w_v[pl.ds(row0, 64), :]
    for step in range(2):
        part = nn(w_rows, d_v[step])
        for half in range(2):
            m_part[2 * step + half] = part[:, half * 512 : half * 512 + 512].astype(BF)
    pl.semaphore_wait(barrier, 17)

    def m_spread(view, land, send, recv):
        copies = []
        for n, (o, at, rows) in enumerate(
            ((1, 1, (0, 64)), (7, 3, (0, 64)), (2, 2, (0, 32)), (6, 2, (32, 32)))
        ):
            there = land(o, rows)
            copies.append(push(view(at, rows), there, send.at[n], recv.at[n], z_device(o)))
        return copies

    m_rs = m_spread(
        lambda at, rows: m_part.at[(s + at) % 4, pl.ds(*rows)],
        lambda o, rows: m_recv.at[{1: 0, 7: 1, 2: 2, 6: 2}[o], pl.ds(*rows)],
        mr_s, mr_r,
    )
    qkv = []

    def spread(n, src, dst):
        for o in ring:
            at = n * 3 + o - 1
            there = src.at[0, :, cols((s + o) % 4)]
            qkv.append(push(there, dst.at[s], qkv_s.at[at], qkv_r.at[at], seq_at(o)))

    spread(0, k, k_all)
    for copy in m_rs:
        copy.wait_recv()
    total = m_part[s].astype(F32)
    for o in ring:
        total += m_recv[o - 1].astype(F32)
    m_own[...] = total.astype(BF)
    m_all[s, pl.ds(row0, 64), :] = m_own[...]
    m_ag = m_spread(
        lambda at, rows: m_own.at[pl.ds(*rows)],
        lambda o, rows: m_all.at[s, pl.ds(pl.multiple_of(row0 + rows[0], 32), rows[1])],
        ma_s, ma_r,
    )
    spread(1, q, q_all)
    for copy in m_ag:
        copy.wait_recv()
    spread(2, v, v_all)
    def m_rows(index):
        return pl.ds(pl.multiple_of((c * 4 + index) * 64, 64), 64)

    m_rings = [
        ring_gather(
            lambda j, half, k=k: m_all.at[2 * k + half, m_rows(j)], y_at, y, my_s.at[k], my_r.at[k]
        )
        for k in range(2)
    ]
    for start, _, _ in m_rings:
        start(0)
        start(1)
    m_c = [[], []]

    def m_across(k, n, index):
        there = m_all.at[2 * k : 2 * k + 2, m_rows(index)]
        m_c[k].append(push(there, there, mc_s.at[4 * k + n], mc_r.at[4 * k + n], core_at))

    def m_near(k):
        m_rings[k][2][2].wait_recv()
        m_across(k, 1, (y + 3) % 4)
        m_rings[k][2][1].wait_recv()
        m_across(k, 2, (y + 1) % 4)

    def m_far(k):
        m_rings[k][2][4].wait_recv()
        m_rings[k][2][5].wait_recv()
        m_across(k, 3, (y + 2) % 4)

    for k in range(2):
        m_across(k, 0, y)
    m_rings[0][1]()

    for copy in loads[2:]:
        copy.wait()
    for copy in qkv[:6]:
        copy.wait_recv()
    for i in range(4):
        kt[:, i * 256 : i * 256 + 256] = transposed(k_all[i])
    visible = lax.broadcasted_iota(jnp.int32, (256, 256), 0) <= lax.broadcasted_iota(
        jnp.int32, (256, 256), 1
    )
    for i in range(4):
        kk = (i + 1) * 256
        st = nt(k_all[0 : i + 1].reshape(kk, HD), q_all[i])
        diagonal = jnp.where(visible, st[i * 256 :], -1e30)
        st = diagonal if i == 0 else jnp.concatenate([st[: i * 256], diagonal], axis=0)
        top = jnp.max(st, axis=0, keepdims=True)
        e = jnp.exp2((st - top) * (SCALE * LOG2E))
        inverse = 1.0 / jnp.sum(e, axis=0, keepdims=True)
        p_t[i, 0:kk] = (e * inverse).astype(BF)
    m_rings[1][1]()
    m_near(0)
    for copy in qkv[6:]:
        copy.wait_recv()
    for i in range(4):
        vt[:, i * 256 : i * 256 + 256] = transposed(v_all[i])
    for i in range(4):
        kk = (i + 1) * 256
        a_loc[i] = jnp.transpose(nn(vt[:, 0:kk], p_t[i, 0:kk])).astype(BF).reshape(4, 64, HD)
    h_order = [(h + o) % 4 for o in (2, 3, 1, 0)]
    a_cp = []
    for n, a in enumerate(h_order):
        a_r[a, s] = a_loc[a, s]
        for o in ring:
            at = n * 3 + o - 1
            a_cp.append(
                push(a_loc.at[a, (s + o) % 4], a_r.at[a, s], a_s.at[at], a_rs.at[at], seq_at(o))
            )

    m_far(0)
    m_near(1)
    for copy in m_c[0]:
        copy.wait_recv()

    x_rings = [
        ring_sum(
            lambda j, half, k=k: xp.at[j, 2 * k + half], x_land.at[k], head_at, h, x_s.at[k], x_r.at[k]
        )
        for k in range(2)
    ]

    def x_rows(n, step):
        a = h_order[n]
        for t in (2 * step, 2 * step + 1):
            xp[a, t] = nn(af[a], m_all[t]).astype(BF)
        if n < 3:
            x_rings[step][n]()

    for n, a in enumerate(h_order):
        for copy in a_cp[3 * n : 3 * n + 3]:
            copy.wait_recv()
        for src in range(4):
            af[a, :, src * HD : src * HD + HD] = a_r[a, src]
        x_rows(n, 0)
    m_far(1)
    for copy in m_c[1]:
        copy.wait_recv()
    x_rows(0, 1)
    x_rings[0][3]()
    for n in (1, 2, 3):
        x_rows(n, 1)
    for step in range(2):
        pe_w[step] = pe_v[:, step, :].astype(F32)
        ct_w[step] = ct_v[:, step, :].astype(F32)
    for i in range(2):
        at = transposed(af[:, :, i * 256 : i * 256 + 256].reshape(256, 256))
        aft[i] = at.reshape(4, 64, 256)
    gx_rings = [
        ring_gather(
            lambda j, half, k=k: gx_all.at[j, 2 * k + half], head_at, h, gx_s.at[k], gx_r.at[k]
        )
        for k in range(2)
    ]
    for step in range(2):
        if step == 0:
            x_rings[1][3]()
        x = jnp.concatenate([x_rings[step][4](half) for half in range(2)], axis=1) + pe_w[step]
        r = lax.rsqrt(jnp.mean(x * x, axis=-1, keepdims=True) + 1e-05)
        normed = x * r
        co = ct_w[step]
        gx = r * (co - normed * jnp.mean(co * normed, axis=-1, keepdims=True))
        for half in range(2):
            gx_all[h, 2 * step + half] = gx[:, half * 512 : half * 512 + 512].astype(BF)
            gx_rings[step][0](half)

    def gx_wait(*which):
        for ring_of in gx_rings:
            for n in which:
                ring_of[2][n].wait_recv()

    ga_cp = []

    def grad_rows(n, a):
        ga = jnp.zeros((64, 512), F32)
        for t in range(4):
            ga += nt(gx_all[a, t], m_all[t])
        for src in range(4):
            ga_f[a, src] = ga[:, src * HD : src * HD + HD].astype(BF)
        ga_h[a, s] = ga_f[a, s]
        for o in ring:
            at = n * 3 + o - 1
            ga_cp.append(
                push(ga_f.at[a, (s + o) % 4], ga_h.at[a, s], ga_s.at[at], ga_r.at[at], seq_at(o))
            )

    grad_rows(0, h)
    for ring_of in gx_rings:
        ring_of[1]()
    gx_wait(2)
    grad_rows(1, (h + 3) % 4)
    gx_wait(1)
    grad_rows(2, (h + 1) % 4)
    gx_wait(4, 5)
    grad_rows(3, (h + 2) % 4)

    y_order = [(y + o) % 4 for o in (2, 3, 1, 0)]

    def g_rows(core, index, t):
        return nn(aft[core, index], gx_all[:, t].reshape(256, 512))

    g1 = []
    for n, index in enumerate(y_order):
        for t in range(4):
            g_send[index, t] = g_rows(1 - c, index, t).astype(BF)
        g1.append(push(g_send.at[index], g_r1.at[index], g1_s.at[n], g1_r.at[n], core_at))

    def g_view(j, half, part):
        return g2.at[j, 2 * half : 2 * half + 2, :, part * 256 : part * 256 + 256]

    g_rings = [
        ring_sum(
            lambda j, half, part=part: g_view(j, half, part),
            g_land.at[part], y_at, y, g2_s.at[part], g2_r.at[part],
        )
        for part in range(2)
    ]
    for n, index in enumerate(y_order):
        own = [g_rows(c, index, t) for t in range(4)]
        g1[n].wait_recv()
        for t in range(4):
            g2[index, t] = (own[t] + g_r1[index, t].astype(F32)).astype(BF)
        if n == 0:
            g_rings[0][0]()
            g_rings[1][0]()
    for copy in ga_cp:
        copy.wait_recv()
    g_rings[0][1]()
    g_rings[0][2]()

    def backward(i):
        kk = (i + 1) * 256
        ga_i = ga_h[i].reshape(256, HD)
        dpt = nt(v_all[0 : i + 1].reshape(kk, HD), ga_i)
        a_i = a_loc[i].reshape(256, HD)
        delta = jnp.sum(jnp.transpose(ga_i.astype(F32) * a_i.astype(F32)), axis=0, keepdims=True)
        p = p_t[i, 0:kk]
        ds = (p.astype(F32) * (dpt - delta)).astype(BF)
        dv_i, dk_i = nn(p, ga_i), nn(ds, q_all[i])
        if i == 3:
            dv_acc[...] = dv_i
            dk_acc[...] = dk_i
        else:
            dv_acc[0:kk] += dv_i
            dk_acc[0:kk] += dk_i
        dq_b[i] = (jnp.transpose(nn(kt[:, 0:kk], ds)) * SCALE).astype(BF)
        dk_b[i] = (dk_acc[i * 256 : kk] * SCALE).astype(BF)
        dv_b[i] = dv_acc[i * 256 : kk].astype(BF)


    for i in (3, 2, 1, 0):
        backward(i)
    outs = ((dq_b, dq), (dk_b, dk), (dv_b, dv))
    out_cp, out_own = [], []

    def give(n):
        src, dst = outs[n]
        there = dst.at[0, :, cols(s)]
        for o in ring:
            at = n * 3 + o - 1
            out_cp.append(push(src.at[(s + o) % 4], there, o_s.at[at], o_r.at[at], seq_at(o)))
        out_own.append(pltpu.make_async_copy(src.at[s], there, loc.at[16 + n]))
        out_own[-1].start()

    g_rings[0][3]()
    g_rings[1][1]()
    g_rings[1][2]()
    give(0)
    g_rings[1][3]()
    g3c = []
    for part in range(2):
        for half in range(2):
            total = g_rings[part][4](half).astype(BF)
            for t in range(2):
                g3[part, :, 2 * half + t] = total[t].reshape(2, 32, 256)
        for o in range(1, 8):
            oz, os = z_at(o)
            at = part * 7 + o - 1
            g3c.append(
                push(g3.at[part, oz, os], g_r3.at[at], g3_s.at[at], g3_r.at[at], z_device(o))
            )
    g4c = []
    for part in range(2):
        total = g3[part, zh, s].astype(F32)
        for o in range(1, 8):
            g3c[part * 7 + o - 1].wait_recv()
            total += g_r3[part * 7 + o - 1].astype(F32)
        grow[part, s, zh] = total.astype(BF)
        here = grow.at[part, s, zh]
        for o in range(1, 8):
            at = part * 7 + o - 1
            g4c.append(push(here, here, g4_s.at[at], g4_r.at[at], z_device(o)))
    give(1)
    mine = [jnp.zeros((64, 512), F32) for _ in range(2)]
    for part in range(2):
        for copy in g4c[7 * part : 7 * part + 7]:
            copy.wait_recv()
        for j in range(4):
            there = slice(j * 64, j * 64 + 64)
            pair = [grow[part, 2 * k + zh, :, :, there].reshape(64, 64) for k in range(2)]
            gperm[4 * part + j] = jnp.concatenate(pair, axis=1)
        if part:
            block = c * 4 + y
            gcol[block] = gperm[g % 8]
            gcc = [
                push(
                    gperm.at[(g + o) % 8], gcol.at[block], gc_s.at[o - 1], gc_r.at[o - 1], half_at(o)
                )
                for o in range(1, 8)
            ]
        for t in range(4):
            rows = grow[part, t].reshape(64, 256)
            for half in range(2):
                first = (t % 2) * 512 + part * 256
                depth = d_v[t // 2, half * 512 : half * 512 + 512, first : first + 256]
                mine[half] += nt(rows, depth)
    y_cp = []
    for half in range(2):
        dop[half, m_rows(y)] = mine[half].astype(BF)
        here = dop.at[half, m_rows(y)]
        for o in ring:
            at = half * 3 + o - 1
            y_cp.append(push(here, here, y_s.at[at], y_r.at[at], y_at(o)))
    give(2)

    c1, dw_c = [], []

    def out_across(n, index):
        for half in range(2):
            at = 2 * n + half
            if n:
                y_cp[half * 3 + n - 1].wait_recv()
            here = dop.at[half, m_rows(index)]
            there = dw.at[m_rows(index), half * 512 : half * 512 + 512]
            dw_c.append(pltpu.make_async_copy(here, there, loc.at[8 + at]))
            dw_c[at].start()
            c1.append(push(here, there, c_s.at[at], c_r.at[at], core_at))

    out_across(0, y)
    for copy in gcc:
        copy.wait_recv()
    gct = transposed(gcol[...].reshape(512, HD))
    for j in range(4):
        ddp[j] = nn(gct, w_v[:, j * 256 : j * 256 + 256]).astype(BF)
    hc = [
        push(ddp.at[(h + o) % 4], dd_r.at[o - 1], h_s.at[o - 1], h_r.at[o - 1], head_at(o))
        for o in ring
    ]
    for o in ring:
        out_across(o, (y + 4 - o) % 4)
    for copy in hc:
        copy.wait_recv()
    total = ddp[h].astype(F32)
    for o in ring:
        total += dd_r[o - 1].astype(F32)
    dd_o[...] = total
    dd_c = pltpu.make_async_copy(dd_o, dd, loc.at[7])
    dd_c.start()
    for copy in out_cp:
        copy.wait_recv()
    for copy in out_own:
        copy.wait()
    for copy in c1:
        copy.wait_recv()
    for copy in dw_c:
        copy.wait()
    dd_c.wait()
    for copy in sent:
        copy.wait_send()


def widen(*refs):
    for src, dst in zip(refs[:5], refs[5:]):
        dst[...] = src[...].astype(F32)


def shards(t_query, t_key, t_value, out_proj, depth_in, prev_embed, cotangent):
    vmem = lambda shape, kind=BF: pltpu.VMEM(shape, kind)
    dma = lambda *n: pltpu.SemaphoreType.DMA(n)
    frames = jax.ShapeDtypeStruct((1, 256, 512), BF)
    dq, dk, dv, dw, dd = pl.pallas_call(
        kernel,
        out_shape=(
            frames, frames, frames,
            jax.ShapeDtypeStruct((512, 1024), BF), jax.ShapeDtypeStruct((HD, 256), F32),
        ),
        in_specs=[pl.BlockSpec(memory_space=pl.ANY)] * 7,
        out_specs=[pl.BlockSpec(memory_space=pl.ANY)] * 5,
        scratch_shapes=[
            vmem((4, 256, HD)), vmem((4, 256, HD)), vmem((4, 256, HD)),
            vmem((512, 1024)), vmem((2, 1024, 1024)), vmem((64, 2, 1024)), vmem((64, 2, 1024)),
            vmem((2, 64, 1024), F32), vmem((2, 64, 1024), F32),
            vmem((4, 64, 512)), vmem((3, 64, 512)), vmem((64, 512)), vmem((4, 512, 512)),
            vmem((HD, 1024)), vmem((HD, 1024)), vmem((4, 1024, 256)),
            vmem((4, 4, 64, HD)), vmem((4, 4, 64, HD)), vmem((4, 64, 512)), vmem((2, 4, 64, 256)),
            vmem((4, 4, 64, 512)), vmem((2, 6, 64, 512)), vmem((4, 4, 64, 512)),
            vmem((4, 4, 64, HD)), vmem((4, 4, 64, HD)),
            vmem((1024, HD), F32), vmem((1024, HD), F32),
            vmem((4, 256, HD)), vmem((4, 256, HD)), vmem((4, 256, HD)),
            vmem((4, 4, 64, 512)), vmem((4, 4, 64, 512)), vmem((4, 4, 64, 512)),
            vmem((2, 6, 2, 64, 256)), vmem((2, 2, 4, 32, 256)), vmem((14, 32, 256)),
            vmem((2, 4, 2, 32, 256)), vmem((2, 512, 512)), vmem((8, 64, HD)), vmem((8, 64, HD)),
            vmem((4, HD, 256)), vmem((3, HD, 256)), vmem((HD, 256), F32),
            dma(19), dma(9), dma(9), dma(4), dma(4), dma(4), dma(4), dma(2, 6), dma(2, 6), dma(8), dma(8),
            dma(12), dma(12), dma(2, 6), dma(2, 6), dma(2, 6), dma(2, 6), dma(12), dma(12), dma(9), dma(9),
            dma(4), dma(4), dma(2, 6), dma(2, 6), dma(14), dma(14), dma(14), dma(14), dma(7), dma(7),
            dma(3), dma(3), dma(6), dma(6), dma(8), dma(8),
        ],
        compiler_params=pltpu.CompilerParams(
            collective_id=0, has_side_effects=True, vmem_limit_bytes=60 * 1024 * 1024
        ),
    )(t_query, t_key, t_value, out_proj, depth_in, prev_embed, cotangent)
    wide = lambda *shape: jax.ShapeDtypeStruct(shape, F32)
    tokens = pl.BlockSpec((1, 128, 512), lambda i: (0, i, 0))
    weight = pl.BlockSpec((256, 1024), lambda i: (i, 0))
    depth = pl.BlockSpec((64, 256), lambda i: (i, 0))
    specs = [tokens, tokens, tokens, weight, depth]
    dq, dk, dv, dw, dd = pl.pallas_call(
        widen,
        grid=(2,),
        in_specs=specs,
        out_specs=specs,
        out_shape=(wide(1, 256, 512), wide(1, 256, 512), wide(1, 256, 512), wide(512, 1024), wide(HD, 256)),
        compiler_params=pltpu.CompilerParams(vmem_limit_bytes=60 * 1024 * 1024),
    )(dq, dk, dv, dw, dd)
    return dq, dk, dv, dw, jnp.transpose(dd.reshape(2, 64, 256), (0, 2, 1))


def solution(mesh):
    placed = (
        P("grp", "seq", "head"),
        P("grp", "seq", "head"),
        P("grp", "seq", "head"),
        P("head", "seq"),
        P(None, "seq", None),
        P("grp", "head", "seq", None, None),
        P("grp", "head", "seq", None, None),
    )
    return jax.shard_map(
        shards,
        mesh=mesh,
        in_specs=placed,
        out_specs=(
            P("grp", "seq", "head"),
            P("grp", "seq", "head"),
            P("grp", "seq", "head"),
            P("head", "seq"),
            P(None, ("seq", "head"), "grp"),
        ),
        check_vma=False,
    )
```

```python
import jax
import jax.numpy as jnp
from jax import lax
from jax.experimental import pallas as pl
from jax.experimental.pallas import tpu as pltpu
from jax.sharding import PartitionSpec as P

MESH = pl.DeviceIdType.MESH
HD = 128
BF = jnp.bfloat16
F32 = jnp.float32
SCALE = HD ** (-0.5)
LOG2E = 1.4426950408889634


def nt(a, b):
    return lax.dot_general(a, b, (((1,), (1,)), ((), ())), preferred_element_type=F32)


def nn(a, b):
    return jnp.dot(a, b, preferred_element_type=F32)


def transposed(a):
    return jnp.transpose(a.astype(F32)).astype(BF)


def kernel(
    q, k, v, wo, di, pe, ct,
    dq, dk, dv, dw, dd,
    q_all, k_all, v_all, w_v, d_v, pe_v, ct_v, pe_w, ct_w,
    m_part, m_recv, m_own, m_all,
    vt, kt, p_t, a_loc, a_r, af, aft,
    xp, x_land, gx_all, ga_f, ga_h,
    dk_acc, dv_acc, dq_b, dk_b, dv_b,
    g_send, g_r1, g2, g_land, g3, g_r3, grow, dop, gperm, gcol, ddp, dd_r, dd_o,
    loc, qkv_s, qkv_r, mr_s, mr_r, ma_s, ma_r, my_s, my_r, mc_s, mc_r,
    a_s, a_rs, x_s, x_r, gx_s, gx_r, ga_s, ga_r, o_s, o_r,
    g1_s, g1_r, g2_s, g2_r, g3_s, g3_r, g4_s, g4_r, gc_s, gc_r, h_s, h_r,
    y_s, y_r, c_s, c_r,
):
    g, s, h = lax.axis_index("grp"), lax.axis_index("seq"), lax.axis_index("head")
    zh, y, c = g // 8, (g // 2) % 4, g % 2
    ring = (1, 2, 3)
    seq_at = lambda o: {"seq": (s + o) % 4}
    head_at = lambda o: {"head": (h + o) % 4}
    y_at = lambda o: {"grp": zh * 8 + ((y + o) % 4) * 2 + c}
    core_at = {"grp": zh * 8 + y * 2 + (1 - c)}

    half_at = lambda o: {"grp": zh * 8 + (g + o) % 8}

    def z_at(o):
        other = (zh * 4 + s + o) % 8
        return other // 4, other % 4

    def z_device(o):
        oz, os = z_at(o)
        return {"grp": oz * 8 + y * 2 + c, "seq": os}

    sent = []

    def push(src, dst, send_sem, recv_sem, device):
        copy = pltpu.make_async_remote_copy(
            src_ref=src, dst_ref=dst, send_sem=send_sem, recv_sem=recv_sem,
            device_id=device, device_id_type=MESH,
        )
        copy.start()
        sent.append(copy)
        return copy

    def ring_sum(view, land, at, i, send, recv):
        right, left = (i + 1) % 4, (i + 3) % 4
        copies = {}

        def go(n, j, half, device):
            copies[n] = push(view(j, half), land.at[n], send.at[n], recv.at[n], device)

        def add(n, j, half):
            copies[n].wait_recv()
            here = view(j, half)
            here[...] = (here[...].astype(F32) + land[n].astype(F32)).astype(BF)

        def opposite():
            go(0, (i + 2) % 4, 0, at(1))
            go(1, (i + 2) % 4, 1, at(3))

        def to_left():
            go(2, left, 0, at(3))

        def to_right():
            go(3, right, 1, at(1))

        def relay():
            add(0, right, 0)
            go(4, right, 0, at(1))
            add(1, left, 1)
            go(5, left, 1, at(3))

        def result(half):
            copies[2 + half].wait_recv()
            copies[4 + half].wait_recv()
            total = view(i, half)[...].astype(F32) + land[2 + half].astype(F32)
            return total + land[4 + half].astype(F32)

        return opposite, to_left, to_right, relay, result

    def ring_gather(view, at, i, send, recv):
        copies = {}

        def go(n, j, half, device):
            copies[n] = push(view(j, half), view(j, half), send.at[n], recv.at[n], device)

        def start(half):
            go(2 * half, i, half, at(1))
            go(2 * half + 1, i, half, at(3))

        def relay():
            copies[0].wait_recv()
            go(4, (i + 3) % 4, 0, at(1))
            copies[3].wait_recv()
            go(5, (i + 1) % 4, 1, at(3))

        return start, relay, copies

    def cols(index):
        return pl.ds(pl.multiple_of(index * HD, HD), HD)

    loads = [
        (wo, w_v), (di, d_v), (pe.at[0, 0], pe_v), (ct.at[0, 0], ct_v),
        (q.at[0, :, cols(s)], q_all.at[s]), (k.at[0, :, cols(s)], k_all.at[s]),
        (v.at[0, :, cols(s)], v_all.at[s]),
    ]
    loads = [pltpu.make_async_copy(src, dst, loc.at[i]) for i, (src, dst) in enumerate(loads)]
    for copy in loads:
        copy.start()

    barrier = pltpu.get_barrier_semaphore()
    greet = lambda device: pl.semaphore_signal(barrier, inc=1, device_id=device, device_id_type=MESH)
    for o in ring:
        greet(seq_at(o))
        greet(head_at(o))
    for o in range(1, 8):
        greet(half_at(o))
    for o in range(4):
        greet({"grp": (g + 8) % 16, "seq": (s + o) % 4})

    loads[0].wait()
    loads[1].wait()
    row0 = pl.multiple_of((c * 4 + y) * 64, 64)
    w_rows = w_v[pl.ds(row0, 64), :]
    for step in range(2):
        part = nn(w_rows, d_v[step])
        for half in range(2):
            m_part[2 * step + half] = part[:, half * 512 : half * 512 + 512].astype(BF)
    pl.semaphore_wait(barrier, 17)

    def m_spread(view, land, send, recv):
        copies = []
        for n, (o, at, rows) in enumerate(
            ((1, 1, (0, 64)), (7, 3, (0, 64)), (2, 2, (0, 32)), (6, 2, (32, 32)))
        ):
            there = land(o, rows)
            copies.append(push(view(at, rows), there, send.at[n], recv.at[n], z_device(o)))
        return copies

    m_rs = m_spread(
        lambda at, rows: m_part.at[(s + at) % 4, pl.ds(*rows)],
        lambda o, rows: m_recv.at[{1: 0, 7: 1, 2: 2, 6: 2}[o], pl.ds(*rows)],
        mr_s, mr_r,
    )
    qkv = []

    def spread(n, src, dst):
        for o in (2, 1, 3):
            at = n * 3 + o - 1
            there = src.at[0, :, cols((s + o) % 4)]
            qkv.append(push(there, dst.at[s], qkv_s.at[at], qkv_r.at[at], seq_at(o)))

    spread(0, k, k_all)
    for copy in m_rs:
        copy.wait_recv()
    total = m_part[s].astype(F32)
    for o in ring:
        total += m_recv[o - 1].astype(F32)
    m_own[...] = total.astype(BF)
    m_all[s, pl.ds(row0, 64), :] = m_own[...]
    m_ag = m_spread(
        lambda at, rows: m_own.at[pl.ds(*rows)],
        lambda o, rows: m_all.at[s, pl.ds(pl.multiple_of(row0 + rows[0], 32), rows[1])],
        ma_s, ma_r,
    )
    spread(1, q, q_all)
    for copy in m_ag:
        copy.wait_recv()
    spread(2, v, v_all)
    def m_rows(index):
        return pl.ds(pl.multiple_of((c * 4 + index) * 64, 64), 64)

    m_rings = [
        ring_gather(
            lambda j, half, k=k: m_all.at[2 * k + half, m_rows(j)], y_at, y, my_s.at[k], my_r.at[k]
        )
        for k in range(2)
    ]
    for start, _, _ in m_rings:
        start(0)
        start(1)
    m_c = [[], []]

    def m_across(k, n, index):
        there = m_all.at[2 * k : 2 * k + 2, m_rows(index)]
        m_c[k].append(push(there, there, mc_s.at[4 * k + n], mc_r.at[4 * k + n], core_at))

    def m_near(k):
        m_rings[k][2][2].wait_recv()
        m_across(k, 1, (y + 3) % 4)
        m_rings[k][2][1].wait_recv()
        m_across(k, 2, (y + 1) % 4)

    def m_far(k):
        m_rings[k][2][4].wait_recv()
        m_rings[k][2][5].wait_recv()
        m_across(k, 3, (y + 2) % 4)

    for k in range(2):
        m_across(k, 0, y)
    m_rings[0][1]()

    for copy in loads[2:]:
        copy.wait()
    for copy in qkv[:6]:
        copy.wait_recv()
    for i in range(4):
        kt[:, i * 256 : i * 256 + 256] = transposed(k_all[i])
    visible = lax.broadcasted_iota(jnp.int32, (256, 256), 0) <= lax.broadcasted_iota(
        jnp.int32, (256, 256), 1
    )
    for i in range(4):
        kk = (i + 1) * 256
        st = nt(k_all[0 : i + 1].reshape(kk, HD), q_all[i])
        diagonal = jnp.where(visible, st[i * 256 :], -1e30)
        st = diagonal if i == 0 else jnp.concatenate([st[: i * 256], diagonal], axis=0)
        top = jnp.max(st, axis=0, keepdims=True)
        e = jnp.exp2((st - top) * (SCALE * LOG2E))
        inverse = 1.0 / jnp.sum(e, axis=0, keepdims=True)
        p_t[i, 0:kk] = (e * inverse).astype(BF)
    m_rings[1][1]()
    m_near(0)
    for copy in qkv[6:]:
        copy.wait_recv()
    for i in range(4):
        vt[:, i * 256 : i * 256 + 256] = transposed(v_all[i])
    for i in range(4):
        kk = (i + 1) * 256
        a_loc[i] = jnp.transpose(nn(vt[:, 0:kk], p_t[i, 0:kk])).astype(BF).reshape(4, 64, HD)
    h_order = [(h + o) % 4 for o in (2, 3, 1, 0)]
    a_cp = []
    for n, a in enumerate(h_order):
        a_r[a, s] = a_loc[a, s]
        for o in (2, 1, 3):
            at = n * 3 + o - 1
            a_cp.append(
                push(a_loc.at[a, (s + o) % 4], a_r.at[a, s], a_s.at[at], a_rs.at[at], seq_at(o))
            )

    m_far(0)
    m_near(1)
    for copy in m_c[0]:
        copy.wait_recv()

    x_rings = [
        ring_sum(
            lambda j, half, k=k: xp.at[j, 2 * k + half], x_land.at[k], head_at, h, x_s.at[k], x_r.at[k]
        )
        for k in range(2)
    ]

    def x_rows(n, step):
        a = h_order[n]
        for t in (2 * step, 2 * step + 1):
            xp[a, t] = nn(af[a], m_all[t]).astype(BF)
        if n < 3:
            x_rings[step][n]()

    for n, a in enumerate(h_order):
        for copy in a_cp[3 * n : 3 * n + 3]:
            copy.wait_recv()
        for src in range(4):
            af[a, :, src * HD : src * HD + HD] = a_r[a, src]
        x_rows(n, 0)
    m_far(1)
    for copy in m_c[1]:
        copy.wait_recv()
    x_rows(0, 1)
    x_rings[0][3]()
    for n in (1, 2, 3):
        x_rows(n, 1)
    for step in range(2):
        pe_w[step] = pe_v[:, step, :].astype(F32)
        ct_w[step] = ct_v[:, step, :].astype(F32)
    for i in range(2):
        at = transposed(af[:, :, i * 256 : i * 256 + 256].reshape(256, 256))
        aft[i] = at.reshape(4, 64, 256)
    gx_rings = [
        ring_gather(
            lambda j, half, k=k: gx_all.at[j, 2 * k + half], head_at, h, gx_s.at[k], gx_r.at[k]
        )
        for k in range(2)
    ]
    for step in range(2):
        if step == 0:
            x_rings[1][3]()
        x = jnp.concatenate([x_rings[step][4](half) for half in range(2)], axis=1) + pe_w[step]
        r = lax.rsqrt(jnp.mean(x * x, axis=-1, keepdims=True) + 1e-05)
        normed = x * r
        co = ct_w[step]
        gx = r * (co - normed * jnp.mean(co * normed, axis=-1, keepdims=True))
        for half in range(2):
            gx_all[h, 2 * step + half] = gx[:, half * 512 : half * 512 + 512].astype(BF)
            gx_rings[step][0](half)

    def gx_wait(*which):
        for ring_of in gx_rings:
            for n in which:
                ring_of[2][n].wait_recv()

    ga_cp = []

    def grad_rows(n, a):
        ga = jnp.zeros((64, 512), F32)
        for t in range(4):
            ga += nt(gx_all[a, t], m_all[t])
        for src in range(4):
            ga_f[a, src] = ga[:, src * HD : src * HD + HD].astype(BF)
        ga_h[a, s] = ga_f[a, s]
        for o in ring:
            at = n * 3 + o - 1
            ga_cp.append(
                push(ga_f.at[a, (s + o) % 4], ga_h.at[a, s], ga_s.at[at], ga_r.at[at], seq_at(o))
            )

    grad_rows(0, h)
    for ring_of in gx_rings:
        ring_of[1]()
    gx_wait(2)
    grad_rows(1, (h + 3) % 4)
    gx_wait(1)
    grad_rows(2, (h + 1) % 4)
    gx_wait(4, 5)

    y_order = [(y + o) % 4 for o in (2, 3, 1, 0)]

    def g_rows(core, index, t):
        return nn(aft[core, index], gx_all[:, t].reshape(256, 512))

    g1 = []
    for n, index in enumerate(y_order):
        for t in range(4):
            g_send[index, t] = g_rows(1 - c, index, t).astype(BF)
        g1.append(push(g_send.at[index], g_r1.at[index], g1_s.at[n], g1_r.at[n], core_at))
    grad_rows(3, (h + 2) % 4)

    def g_view(j, half, part):
        return g2.at[j, 2 * half : 2 * half + 2, :, part * 256 : part * 256 + 256]

    g_rings = [
        ring_sum(
            lambda j, half, part=part: g_view(j, half, part),
            g_land.at[part], y_at, y, g2_s.at[part], g2_r.at[part],
        )
        for part in range(2)
    ]
    for n, index in enumerate(y_order):
        own = [g_rows(c, index, t) for t in range(4)]
        g1[n].wait_recv()
        for t in range(4):
            g2[index, t] = (own[t] + g_r1[index, t].astype(F32)).astype(BF)
        if n == 0:
            g_rings[0][0]()
            g_rings[1][0]()
    for copy in ga_cp:
        copy.wait_recv()
    g_rings[0][1]()
    g_rings[0][2]()

    def backward(i):
        kk = (i + 1) * 256
        ga_i = ga_h[i].reshape(256, HD)
        dpt = nt(v_all[0 : i + 1].reshape(kk, HD), ga_i)
        a_i = a_loc[i].reshape(256, HD)
        delta = jnp.sum(jnp.transpose(ga_i.astype(F32) * a_i.astype(F32)), axis=0, keepdims=True)
        p = p_t[i, 0:kk]
        ds = (p.astype(F32) * (dpt - delta)).astype(BF)
        dv_i, dk_i = nn(p, ga_i), nn(ds, q_all[i])
        if i == 3:
            dv_acc[...] = dv_i
            dk_acc[...] = dk_i
        else:
            dv_acc[0:kk] += dv_i
            dk_acc[0:kk] += dk_i
        dq_b[i] = (jnp.transpose(nn(kt[:, 0:kk], ds)) * SCALE).astype(BF)
        dk_b[i] = (dk_acc[i * 256 : kk] * SCALE).astype(BF)
        dv_b[i] = dv_acc[i * 256 : kk].astype(BF)


    for i in (3, 2, 1, 0):
        backward(i)
    outs = ((dq_b, dq), (dk_b, dk), (dv_b, dv))
    out_cp, out_own = [], []

    def give(n):
        src, dst = outs[n]
        there = dst.at[0, :, cols(s)]
        for o in (2, 1, 3):
            at = n * 3 + o - 1
            out_cp.append(push(src.at[(s + o) % 4], there, o_s.at[at], o_r.at[at], seq_at(o)))
        out_own.append(pltpu.make_async_copy(src.at[s], there, loc.at[16 + n]))
        out_own[-1].start()

    give(0)
    g_rings[0][3]()
    g_rings[1][1]()
    g_rings[1][2]()
    g_rings[1][3]()
    g3c = []
    for part in range(2):
        for half in range(2):
            total = g_rings[part][4](half).astype(BF)
            for t in range(2):
                g3[part, :, 2 * half + t] = total[t].reshape(2, 32, 256)
        for o in range(1, 8):
            oz, os = z_at(o)
            at = part * 7 + o - 1
            g3c.append(
                push(g3.at[part, oz, os], g_r3.at[at], g3_s.at[at], g3_r.at[at], z_device(o))
            )
    g4c = []
    for part in range(2):
        total = g3[part, zh, s].astype(F32)
        for o in range(1, 8):
            g3c[part * 7 + o - 1].wait_recv()
            total += g_r3[part * 7 + o - 1].astype(F32)
        grow[part, s, zh] = total.astype(BF)
        here = grow.at[part, s, zh]
        for o in range(1, 8):
            at = part * 7 + o - 1
            g4c.append(push(here, here, g4_s.at[at], g4_r.at[at], z_device(o)))
    mine = [jnp.zeros((64, 512), F32) for _ in range(2)]
    for part in range(2):
        for copy in g4c[7 * part : 7 * part + 7]:
            copy.wait_recv()
        for j in range(4):
            there = slice(j * 64, j * 64 + 64)
            pair = [grow[part, 2 * k + zh, :, :, there].reshape(64, 64) for k in range(2)]
            gperm[4 * part + j] = jnp.concatenate(pair, axis=1)
        if part:
            block = c * 4 + y
            gcol[block] = gperm[g % 8]
            gcc = [
                push(
                    gperm.at[(g + o) % 8], gcol.at[block], gc_s.at[o - 1], gc_r.at[o - 1], half_at(o)
                )
                for o in range(1, 8)
            ]
        for t in range(4):
            rows = grow[part, t].reshape(64, 256)
            for half in range(2):
                first = (t % 2) * 512 + part * 256
                depth = d_v[t // 2, half * 512 : half * 512 + 512, first : first + 256]
                mine[half] += nt(rows, depth)
    y_cp = []
    for half in range(2):
        dop[half, m_rows(y)] = mine[half].astype(BF)
        here = dop.at[half, m_rows(y)]
        for o in ring:
            at = half * 3 + o - 1
            y_cp.append(push(here, here, y_s.at[at], y_r.at[at], y_at(o)))
    give(1)
    give(2)

    c1, dw_c = [], []

    def out_across(n, index):
        for half in range(2):
            at = 2 * n + half
            if n:
                y_cp[half * 3 + n - 1].wait_recv()
            here = dop.at[half, m_rows(index)]
            there = dw.at[m_rows(index), half * 512 : half * 512 + 512]
            dw_c.append(pltpu.make_async_copy(here, there, loc.at[8 + at]))
            dw_c[at].start()
            c1.append(push(here, there, c_s.at[at], c_r.at[at], core_at))

    out_across(0, y)
    for copy in gcc:
        copy.wait_recv()
    gct = transposed(gcol[...].reshape(512, HD))
    for j in range(4):
        ddp[j] = nn(gct, w_v[:, j * 256 : j * 256 + 256]).astype(BF)
    hc = [
        push(ddp.at[(h + o) % 4], dd_r.at[o - 1], h_s.at[o - 1], h_r.at[o - 1], head_at(o))
        for o in ring
    ]
    for o in ring:
        out_across(o, (y + 4 - o) % 4)
    for copy in hc:
        copy.wait_recv()
    total = ddp[h].astype(F32)
    for o in ring:
        total += dd_r[o - 1].astype(F32)
    dd_o[...] = total
    dd_c = pltpu.make_async_copy(dd_o, dd, loc.at[7])
    dd_c.start()
    for copy in out_cp:
        copy.wait_recv()
    for copy in out_own:
        copy.wait()
    for copy in c1:
        copy.wait_recv()
    for copy in dw_c:
        copy.wait()
    dd_c.wait()
    for copy in sent:
        copy.wait_send()


def widen(*refs):
    for src, dst in zip(refs[:5], refs[5:]):
        dst[...] = src[...].astype(F32)


def shards(t_query, t_key, t_value, out_proj, depth_in, prev_embed, cotangent):
    vmem = lambda shape, kind=BF: pltpu.VMEM(shape, kind)
    dma = lambda *n: pltpu.SemaphoreType.DMA(n)
    frames = jax.ShapeDtypeStruct((1, 256, 512), BF)
    dq, dk, dv, dw, dd = pl.pallas_call(
        kernel,
        out_shape=(
            frames, frames, frames,
            jax.ShapeDtypeStruct((512, 1024), BF), jax.ShapeDtypeStruct((HD, 256), F32),
        ),
        in_specs=[pl.BlockSpec(memory_space=pl.ANY)] * 7,
        out_specs=[pl.BlockSpec(memory_space=pl.ANY)] * 5,
        scratch_shapes=[
            vmem((4, 256, HD)), vmem((4, 256, HD)), vmem((4, 256, HD)),
            vmem((512, 1024)), vmem((2, 1024, 1024)), vmem((64, 2, 1024)), vmem((64, 2, 1024)),
            vmem((2, 64, 1024), F32), vmem((2, 64, 1024), F32),
            vmem((4, 64, 512)), vmem((3, 64, 512)), vmem((64, 512)), vmem((4, 512, 512)),
            vmem((HD, 1024)), vmem((HD, 1024)), vmem((4, 1024, 256)),
            vmem((4, 4, 64, HD)), vmem((4, 4, 64, HD)), vmem((4, 64, 512)), vmem((2, 4, 64, 256)),
            vmem((4, 4, 64, 512)), vmem((2, 6, 64, 512)), vmem((4, 4, 64, 512)),
            vmem((4, 4, 64, HD)), vmem((4, 4, 64, HD)),
            vmem((1024, HD), F32), vmem((1024, HD), F32),
            vmem((4, 256, HD)), vmem((4, 256, HD)), vmem((4, 256, HD)),
            vmem((4, 4, 64, 512)), vmem((4, 4, 64, 512)), vmem((4, 4, 64, 512)),
            vmem((2, 6, 2, 64, 256)), vmem((2, 2, 4, 32, 256)), vmem((14, 32, 256)),
            vmem((2, 4, 2, 32, 256)), vmem((2, 512, 512)), vmem((8, 64, HD)), vmem((8, 64, HD)),
            vmem((4, HD, 256)), vmem((3, HD, 256)), vmem((HD, 256), F32),
            dma(19), dma(9), dma(9), dma(4), dma(4), dma(4), dma(4), dma(2, 6), dma(2, 6), dma(8), dma(8),
            dma(12), dma(12), dma(2, 6), dma(2, 6), dma(2, 6), dma(2, 6), dma(12), dma(12), dma(9), dma(9),
            dma(4), dma(4), dma(2, 6), dma(2, 6), dma(14), dma(14), dma(14), dma(14), dma(7), dma(7),
            dma(3), dma(3), dma(6), dma(6), dma(8), dma(8),
        ],
        compiler_params=pltpu.CompilerParams(
            collective_id=0, has_side_effects=True, vmem_limit_bytes=60 * 1024 * 1024
        ),
    )(t_query, t_key, t_value, out_proj, depth_in, prev_embed, cotangent)
    wide = lambda *shape: jax.ShapeDtypeStruct(shape, F32)
    tokens = pl.BlockSpec((1, 128, 512), lambda i: (0, i, 0))
    weight = pl.BlockSpec((256, 1024), lambda i: (i, 0))
    depth = pl.BlockSpec((64, 256), lambda i: (i, 0))
    specs = [tokens, tokens, tokens, weight, depth]
    dq, dk, dv, dw, dd = pl.pallas_call(
        widen,
        grid=(2,),
        in_specs=specs,
        out_specs=specs,
        out_shape=(wide(1, 256, 512), wide(1, 256, 512), wide(1, 256, 512), wide(512, 1024), wide(HD, 256)),
        compiler_params=pltpu.CompilerParams(vmem_limit_bytes=60 * 1024 * 1024),
    )(dq, dk, dv, dw, dd)
    return dq, dk, dv, dw, jnp.transpose(dd.reshape(2, 64, 256), (0, 2, 1))


def solution(mesh):
    placed = (
        P("grp", "seq", "head"),
        P("grp", "seq", "head"),
        P("grp", "seq", "head"),
        P("head", "seq"),
        P(None, "seq", None),
        P("grp", "head", "seq", None, None),
        P("grp", "head", "seq", None, None),
    )
    return jax.shard_map(
        shards,
        mesh=mesh,
        in_specs=placed,
        out_specs=(
            P("grp", "seq", "head"),
            P("grp", "seq", "head"),
            P("grp", "seq", "head"),
            P("head", "seq"),
            P(None, ("seq", "head"), "grp"),
        ),
        check_vma=False,
    )
```

```python
import jax
import jax.numpy as jnp
from jax import lax
from jax.experimental import pallas as pl
from jax.experimental.pallas import tpu as pltpu
from jax.sharding import PartitionSpec as P

MESH = pl.DeviceIdType.MESH
HD = 128
BF = jnp.bfloat16
F32 = jnp.float32
SCALE = HD ** (-0.5)
LOG2E = 1.4426950408889634


def nt(a, b):
    return lax.dot_general(a, b, (((1,), (1,)), ((), ())), preferred_element_type=F32)


def nn(a, b):
    return jnp.dot(a, b, preferred_element_type=F32)


def transposed(a):
    return jnp.transpose(a.astype(F32)).astype(BF)


def kernel(
    q, k, v, wo, di, pe, ct,
    dq, dk, dv, dw, dd,
    q_all, k_all, v_all, w_v, d_v, pe_v, ct_v, pe_w, ct_w,
    m_part, m_recv, m_own, m_all,
    vt, kt, p_t, a_loc, a_r, af, aft,
    xp, x_land, gx_all, ga_f, ga_h,
    dk_acc, dv_acc, dq_b, dk_b, dv_b,
    g_send, g_r1, g2, g_land, g3, g_r3, grow, dop, gperm, gcol, ddp, dd_r, dd_o,
    loc, qkv_s, qkv_r, mr_s, mr_r, ma_s, ma_r, my_s, my_r, mc_s, mc_r,
    a_s, a_rs, x_s, x_r, gx_s, gx_r, ga_s, ga_r, o_s, o_r,
    g1_s, g1_r, g2_s, g2_r, g3_s, g3_r, g4_s, g4_r, gc_s, gc_r, h_s, h_r,
    y_s, y_r, c_s, c_r,
):
    g, s, h = lax.axis_index("grp"), lax.axis_index("seq"), lax.axis_index("head")
    zh, y, c = g // 8, (g // 2) % 4, g % 2
    ring = (1, 2, 3)
    seq_at = lambda o: {"seq": (s + o) % 4}
    head_at = lambda o: {"head": (h + o) % 4}
    y_at = lambda o: {"grp": zh * 8 + ((y + o) % 4) * 2 + c}
    core_at = {"grp": zh * 8 + y * 2 + (1 - c)}

    half_at = lambda o: {"grp": zh * 8 + (g + o) % 8}

    def z_at(o):
        other = (zh * 4 + s + o) % 8
        return other // 4, other % 4

    def z_device(o):
        oz, os = z_at(o)
        return {"grp": oz * 8 + y * 2 + c, "seq": os}

    sent = []

    def push(src, dst, send_sem, recv_sem, device):
        copy = pltpu.make_async_remote_copy(
            src_ref=src, dst_ref=dst, send_sem=send_sem, recv_sem=recv_sem,
            device_id=device, device_id_type=MESH,
        )
        copy.start()
        sent.append(copy)
        return copy

    def ring_sum(view, land, at, i, send, recv):
        right, left = (i + 1) % 4, (i + 3) % 4
        copies = {}

        def go(n, j, half, device):
            copies[n] = push(view(j, half), land.at[n], send.at[n], recv.at[n], device)

        def add(n, j, half):
            copies[n].wait_recv()
            here = view(j, half)
            here[...] = (here[...].astype(F32) + land[n].astype(F32)).astype(BF)

        def opposite():
            go(0, (i + 2) % 4, 0, at(1))
            go(1, (i + 2) % 4, 1, at(3))

        def to_left():
            go(2, left, 0, at(3))

        def to_right():
            go(3, right, 1, at(1))

        def relay():
            add(0, right, 0)
            go(4, right, 0, at(1))
            add(1, left, 1)
            go(5, left, 1, at(3))

        def result(half):
            copies[2 + half].wait_recv()
            copies[4 + half].wait_recv()
            total = view(i, half)[...].astype(F32) + land[2 + half].astype(F32)
            return total + land[4 + half].astype(F32)

        return opposite, to_left, to_right, relay, result

    def ring_gather(view, at, i, send, recv):
        copies = {}

        def go(n, j, half, device):
            copies[n] = push(view(j, half), view(j, half), send.at[n], recv.at[n], device)

        def start(half):
            go(2 * half, i, half, at(1))
            go(2 * half + 1, i, half, at(3))

        def relay():
            copies[0].wait_recv()
            go(4, (i + 3) % 4, 0, at(1))
            copies[3].wait_recv()
            go(5, (i + 1) % 4, 1, at(3))

        return start, relay, copies

    def cols(index):
        return pl.ds(pl.multiple_of(index * HD, HD), HD)

    loads = [
        (wo, w_v), (di, d_v), (pe.at[0, 0], pe_v), (ct.at[0, 0], ct_v),
        (q.at[0, :, cols(s)], q_all.at[s]), (k.at[0, :, cols(s)], k_all.at[s]),
        (v.at[0, :, cols(s)], v_all.at[s]),
    ]
    loads = [pltpu.make_async_copy(src, dst, loc.at[i]) for i, (src, dst) in enumerate(loads)]
    for copy in loads:
        copy.start()

    barrier = pltpu.get_barrier_semaphore()
    greet = lambda device: pl.semaphore_signal(barrier, inc=1, device_id=device, device_id_type=MESH)
    for o in ring:
        greet(seq_at(o))
        greet(head_at(o))
    for o in range(1, 8):
        greet(half_at(o))
    for o in range(4):
        greet({"grp": (g + 8) % 16, "seq": (s + o) % 4})

    loads[0].wait()
    loads[1].wait()
    row0 = pl.multiple_of((c * 4 + y) * 64, 64)
    w_rows = w_v[pl.ds(row0, 64), :]
    for step in range(2):
        part = nn(w_rows, d_v[step])
        for half in range(2):
            m_part[2 * step + half] = part[:, half * 512 : half * 512 + 512].astype(BF)
    pl.semaphore_wait(barrier, 17)

    def m_spread(view, land, send, recv):
        copies = []
        for n, (o, at, rows) in enumerate(
            ((1, 1, (0, 64)), (7, 3, (0, 64)), (2, 2, (0, 32)), (6, 2, (32, 32)))
        ):
            there = land(o, rows)
            copies.append(push(view(at, rows), there, send.at[n], recv.at[n], z_device(o)))
        return copies

    m_rs = m_spread(
        lambda at, rows: m_part.at[(s + at) % 4, pl.ds(*rows)],
        lambda o, rows: m_recv.at[{1: 0, 7: 1, 2: 2, 6: 2}[o], pl.ds(*rows)],
        mr_s, mr_r,
    )
    qkv = []

    def spread(n, src, dst):
        for o in (2, 1, 3):
            at = n * 3 + o - 1
            there = src.at[0, :, cols((s + o) % 4)]
            qkv.append(push(there, dst.at[s], qkv_s.at[at], qkv_r.at[at], seq_at(o)))

    spread(0, k, k_all)
    for copy in m_rs:
        copy.wait_recv()
    total = m_part[s].astype(F32)
    for o in ring:
        total += m_recv[o - 1].astype(F32)
    m_own[...] = total.astype(BF)
    m_all[s, pl.ds(row0, 64), :] = m_own[...]
    m_ag = m_spread(
        lambda at, rows: m_own.at[pl.ds(*rows)],
        lambda o, rows: m_all.at[s, pl.ds(pl.multiple_of(row0 + rows[0], 32), rows[1])],
        ma_s, ma_r,
    )
    spread(1, q, q_all)
    for copy in m_ag:
        copy.wait_recv()
    spread(2, v, v_all)
    def m_rows(index):
        return pl.ds(pl.multiple_of((c * 4 + index) * 64, 64), 64)

    m_rings = [
        ring_gather(
            lambda j, half, k=k: m_all.at[2 * k + half, m_rows(j)], y_at, y, my_s.at[k], my_r.at[k]
        )
        for k in range(2)
    ]
    for start, _, _ in m_rings:
        start(0)
        start(1)
    m_c = [[], []]

    def m_across(k, n, index):
        there = m_all.at[2 * k : 2 * k + 2, m_rows(index)]
        m_c[k].append(push(there, there, mc_s.at[4 * k + n], mc_r.at[4 * k + n], core_at))

    def m_near(k):
        m_rings[k][2][2].wait_recv()
        m_across(k, 1, (y + 3) % 4)
        m_rings[k][2][1].wait_recv()
        m_across(k, 2, (y + 1) % 4)

    def m_far(k):
        m_rings[k][2][4].wait_recv()
        m_rings[k][2][5].wait_recv()
        m_across(k, 3, (y + 2) % 4)

    for k in range(2):
        m_across(k, 0, y)
    m_rings[0][1]()

    for copy in loads[2:]:
        copy.wait()
    for copy in qkv[:6]:
        copy.wait_recv()
    for i in range(4):
        kt[:, i * 256 : i * 256 + 256] = transposed(k_all[i])
    visible = lax.broadcasted_iota(jnp.int32, (256, 256), 0) <= lax.broadcasted_iota(
        jnp.int32, (256, 256), 1
    )
    for i in range(4):
        kk = (i + 1) * 256
        st = nt(k_all[0 : i + 1].reshape(kk, HD), q_all[i])
        diagonal = jnp.where(visible, st[i * 256 :], -1e30)
        st = diagonal if i == 0 else jnp.concatenate([st[: i * 256], diagonal], axis=0)
        top = jnp.max(st, axis=0, keepdims=True)
        e = jnp.exp2((st - top) * (SCALE * LOG2E))
        inverse = 1.0 / jnp.sum(e, axis=0, keepdims=True)
        p_t[i, 0:kk] = (e * inverse).astype(BF)
    m_rings[1][1]()
    m_near(0)
    for copy in qkv[6:]:
        copy.wait_recv()
    for i in range(4):
        vt[:, i * 256 : i * 256 + 256] = transposed(v_all[i])
    for i in range(4):
        kk = (i + 1) * 256
        a_loc[i] = jnp.transpose(nn(vt[:, 0:kk], p_t[i, 0:kk])).astype(BF).reshape(4, 64, HD)
    h_order = [(h + o) % 4 for o in (2, 3, 1, 0)]
    a_cp = []
    for n, a in enumerate(h_order):
        a_r[a, s] = a_loc[a, s]
        for o in (2, 1, 3):
            at = n * 3 + o - 1
            a_cp.append(
                push(a_loc.at[a, (s + o) % 4], a_r.at[a, s], a_s.at[at], a_rs.at[at], seq_at(o))
            )

    m_far(0)
    m_near(1)
    for copy in m_c[0]:
        copy.wait_recv()

    x_rings = [
        ring_sum(
            lambda j, half, k=k: xp.at[j, 2 * k + half], x_land.at[k], head_at, h, x_s.at[k], x_r.at[k]
        )
        for k in range(2)
    ]

    def x_rows(n, step):
        a = h_order[n]
        for t in (2 * step, 2 * step + 1):
            xp[a, t] = nn(af[a], m_all[t]).astype(BF)
        if n < 3:
            x_rings[step][n]()

    for n, a in enumerate(h_order):
        for copy in a_cp[3 * n : 3 * n + 3]:
            copy.wait_recv()
        for src in range(4):
            af[a, :, src * HD : src * HD + HD] = a_r[a, src]
        x_rows(n, 0)
    m_far(1)
    for copy in m_c[1]:
        copy.wait_recv()
    x_rows(0, 1)
    x_rings[0][3]()
    for n in (1, 2, 3):
        x_rows(n, 1)
    for step in range(2):
        pe_w[step] = pe_v[:, step, :].astype(F32)
        ct_w[step] = ct_v[:, step, :].astype(F32)
    for i in range(2):
        at = transposed(af[:, :, i * 256 : i * 256 + 256].reshape(256, 256))
        aft[i] = at.reshape(4, 64, 256)
    gx_rings = [
        ring_gather(
            lambda j, half, k=k: gx_all.at[j, 2 * k + half], head_at, h, gx_s.at[k], gx_r.at[k]
        )
        for k in range(2)
    ]
    for step in range(2):
        if step == 0:
            x_rings[1][3]()
        x = jnp.concatenate([x_rings[step][4](half) for half in range(2)], axis=1) + pe_w[step]
        r = lax.rsqrt(jnp.mean(x * x, axis=-1, keepdims=True) + 1e-05)
        normed = x * r
        co = ct_w[step]
        gx = r * (co - normed * jnp.mean(co * normed, axis=-1, keepdims=True))
        for half in range(2):
            gx_all[h, 2 * step + half] = gx[:, half * 512 : half * 512 + 512].astype(BF)
            gx_rings[step][0](half)

    def gx_wait(*which):
        for ring_of in gx_rings:
            for n in which:
                ring_of[2][n].wait_recv()

    ga_cp = []

    def grad_rows(n, a):
        ga = jnp.zeros((64, 512), F32)
        for t in range(4):
            ga += nt(gx_all[a, t], m_all[t])
        for src in range(4):
            ga_f[a, src] = ga[:, src * HD : src * HD + HD].astype(BF)
        ga_h[a, s] = ga_f[a, s]
        for o in (2, 1, 3):
            at = n * 3 + o - 1
            ga_cp.append(
                push(ga_f.at[a, (s + o) % 4], ga_h.at[a, s], ga_s.at[at], ga_r.at[at], seq_at(o))
            )

    grad_rows(0, h)
    for ring_of in gx_rings:
        ring_of[1]()
    gx_wait(2)
    grad_rows(1, (h + 3) % 4)
    gx_wait(1)
    grad_rows(2, (h + 1) % 4)
    gx_wait(4, 5)

    y_order = [(y + o) % 4 for o in (2, 3, 1, 0)]

    def g_rows(core, index, t):
        return nn(aft[core, index], gx_all[:, t].reshape(256, 512))

    g1 = []
    for n, index in enumerate(y_order):
        for t in range(4):
            g_send[index, t] = g_rows(1 - c, index, t).astype(BF)
        g1.append(push(g_send.at[index], g_r1.at[index], g1_s.at[n], g1_r.at[n], core_at))
    grad_rows(3, (h + 2) % 4)

    def g_view(j, half, part):
        return g2.at[j, 2 * half : 2 * half + 2, :, part * 256 : part * 256 + 256]

    g_rings = [
        ring_sum(
            lambda j, half, part=part: g_view(j, half, part),
            g_land.at[part], y_at, y, g2_s.at[part], g2_r.at[part],
        )
        for part in range(2)
    ]
    for n, index in enumerate(y_order):
        own = [g_rows(c, index, t) for t in range(4)]
        g1[n].wait_recv()
        for t in range(4):
            g2[index, t] = (own[t] + g_r1[index, t].astype(F32)).astype(BF)
        if n == 0:
            g_rings[0][0]()
            g_rings[1][0]()
    for copy in ga_cp:
        copy.wait_recv()
    g_rings[0][1]()
    g_rings[0][2]()

    def backward(i):
        kk = (i + 1) * 256
        ga_i = ga_h[i].reshape(256, HD)
        dpt = nt(v_all[0 : i + 1].reshape(kk, HD), ga_i)
        a_i = a_loc[i].reshape(256, HD)
        delta = jnp.sum(jnp.transpose(ga_i.astype(F32) * a_i.astype(F32)), axis=0, keepdims=True)
        p = p_t[i, 0:kk]
        ds = (p.astype(F32) * (dpt - delta)).astype(BF)
        dv_i, dk_i = nn(p, ga_i), nn(ds, q_all[i])
        if i == 3:
            dv_acc[...] = dv_i
            dk_acc[...] = dk_i
        else:
            dv_acc[0:kk] += dv_i
            dk_acc[0:kk] += dk_i
        dq_b[i] = (jnp.transpose(nn(kt[:, 0:kk], ds)) * SCALE).astype(BF)
        dk_b[i] = (dk_acc[i * 256 : kk] * SCALE).astype(BF)
        dv_b[i] = dv_acc[i * 256 : kk].astype(BF)


    for i in (3, 2, 1, 0):
        backward(i)
    outs = ((dq_b, dq), (dk_b, dk), (dv_b, dv))
    out_cp, out_own = [], []

    def give(n):
        src, dst = outs[n]
        there = dst.at[0, :, cols(s)]
        for o in (2, 1, 3):
            at = n * 3 + o - 1
            out_cp.append(push(src.at[(s + o) % 4], there, o_s.at[at], o_r.at[at], seq_at(o)))
        out_own.append(pltpu.make_async_copy(src.at[s], there, loc.at[16 + n]))
        out_own[-1].start()

    give(0)
    g_rings[0][3]()
    g_rings[1][1]()
    g_rings[1][2]()
    g_rings[1][3]()
    z_order = (4, 3, 5, 2, 6, 1, 7)
    g3c = {}
    for part in range(2):
        for half in range(2):
            total = g_rings[part][4](half).astype(BF)
            for t in range(2):
                g3[part, :, 2 * half + t] = total[t].reshape(2, 32, 256)
        for o in z_order:
            oz, os = z_at(o)
            at = part * 7 + o - 1
            g3c[at] = push(
                g3.at[part, oz, os], g_r3.at[at], g3_s.at[at], g3_r.at[at], z_device(o)
            )
    g4c = []
    for part in range(2):
        total = g3[part, zh, s].astype(F32)
        for o in range(1, 8):
            g3c[part * 7 + o - 1].wait_recv()
            total += g_r3[part * 7 + o - 1].astype(F32)
        grow[part, s, zh] = total.astype(BF)
        here = grow.at[part, s, zh]
        for o in z_order:
            at = part * 7 + o - 1
            g4c.append(push(here, here, g4_s.at[at], g4_r.at[at], z_device(o)))
    mine = [jnp.zeros((64, 512), F32) for _ in range(2)]
    for part in range(2):
        for copy in g4c[7 * part : 7 * part + 7]:
            copy.wait_recv()
        for j in range(4):
            there = slice(j * 64, j * 64 + 64)
            pair = [grow[part, 2 * k + zh, :, :, there].reshape(64, 64) for k in range(2)]
            gperm[4 * part + j] = jnp.concatenate(pair, axis=1)
        if part:
            block = c * 4 + y
            gcol[block] = gperm[g % 8]
            gcc = [
                push(
                    gperm.at[(g + o) % 8], gcol.at[block], gc_s.at[o - 1], gc_r.at[o - 1], half_at(o)
                )
                for o in range(1, 8)
            ]
        for t in range(4):
            rows = grow[part, t].reshape(64, 256)
            for half in range(2):
                first = (t % 2) * 512 + part * 256
                depth = d_v[t // 2, half * 512 : half * 512 + 512, first : first + 256]
                mine[half] += nt(rows, depth)
    y_cp = []
    for half in range(2):
        dop[half, m_rows(y)] = mine[half].astype(BF)
        here = dop.at[half, m_rows(y)]
        for o in ring:
            at = half * 3 + o - 1
            y_cp.append(push(here, here, y_s.at[at], y_r.at[at], y_at(o)))
    give(1)
    give(2)

    c1, dw_c = [], []

    def out_across(n, index):
        for half in range(2):
            at = 2 * n + half
            if n:
                y_cp[half * 3 + n - 1].wait_recv()
            here = dop.at[half, m_rows(index)]
            there = dw.at[m_rows(index), half * 512 : half * 512 + 512]
            dw_c.append(pltpu.make_async_copy(here, there, loc.at[8 + at]))
            dw_c[at].start()
            c1.append(push(here, there, c_s.at[at], c_r.at[at], core_at))

    out_across(0, y)
    for copy in gcc:
        copy.wait_recv()
    gct = transposed(gcol[...].reshape(512, HD))
    for j in range(4):
        ddp[j] = nn(gct, w_v[:, j * 256 : j * 256 + 256]).astype(BF)
    hc = [
        push(ddp.at[(h + o) % 4], dd_r.at[o - 1], h_s.at[o - 1], h_r.at[o - 1], head_at(o))
        for o in ring
    ]
    for o in ring:
        out_across(o, (y + 4 - o) % 4)
    for copy in hc:
        copy.wait_recv()
    total = ddp[h].astype(F32)
    for o in ring:
        total += dd_r[o - 1].astype(F32)
    dd_o[...] = total
    dd_c = pltpu.make_async_copy(dd_o, dd, loc.at[7])
    dd_c.start()
    for copy in out_cp:
        copy.wait_recv()
    for copy in out_own:
        copy.wait()
    for copy in c1:
        copy.wait_recv()
    for copy in dw_c:
        copy.wait()
    dd_c.wait()
    for copy in sent:
        copy.wait_send()


def widen(*refs):
    for src, dst in zip(refs[:5], refs[5:]):
        dst[...] = src[...].astype(F32)


def shards(t_query, t_key, t_value, out_proj, depth_in, prev_embed, cotangent):
    vmem = lambda shape, kind=BF: pltpu.VMEM(shape, kind)
    dma = lambda *n: pltpu.SemaphoreType.DMA(n)
    frames = jax.ShapeDtypeStruct((1, 256, 512), BF)
    dq, dk, dv, dw, dd = pl.pallas_call(
        kernel,
        out_shape=(
            frames, frames, frames,
            jax.ShapeDtypeStruct((512, 1024), BF), jax.ShapeDtypeStruct((HD, 256), F32),
        ),
        in_specs=[pl.BlockSpec(memory_space=pl.ANY)] * 7,
        out_specs=[pl.BlockSpec(memory_space=pl.ANY)] * 5,
        scratch_shapes=[
            vmem((4, 256, HD)), vmem((4, 256, HD)), vmem((4, 256, HD)),
            vmem((512, 1024)), vmem((2, 1024, 1024)), vmem((64, 2, 1024)), vmem((64, 2, 1024)),
            vmem((2, 64, 1024), F32), vmem((2, 64, 1024), F32),
            vmem((4, 64, 512)), vmem((3, 64, 512)), vmem((64, 512)), vmem((4, 512, 512)),
            vmem((HD, 1024)), vmem((HD, 1024)), vmem((4, 1024, 256)),
            vmem((4, 4, 64, HD)), vmem((4, 4, 64, HD)), vmem((4, 64, 512)), vmem((2, 4, 64, 256)),
            vmem((4, 4, 64, 512)), vmem((2, 6, 64, 512)), vmem((4, 4, 64, 512)),
            vmem((4, 4, 64, HD)), vmem((4, 4, 64, HD)),
            vmem((1024, HD), F32), vmem((1024, HD), F32),
            vmem((4, 256, HD)), vmem((4, 256, HD)), vmem((4, 256, HD)),
            vmem((4, 4, 64, 512)), vmem((4, 4, 64, 512)), vmem((4, 4, 64, 512)),
            vmem((2, 6, 2, 64, 256)), vmem((2, 2, 4, 32, 256)), vmem((14, 32, 256)),
            vmem((2, 4, 2, 32, 256)), vmem((2, 512, 512)), vmem((8, 64, HD)), vmem((8, 64, HD)),
            vmem((4, HD, 256)), vmem((3, HD, 256)), vmem((HD, 256), F32),
            dma(19), dma(9), dma(9), dma(4), dma(4), dma(4), dma(4), dma(2, 6), dma(2, 6), dma(8), dma(8),
            dma(12), dma(12), dma(2, 6), dma(2, 6), dma(2, 6), dma(2, 6), dma(12), dma(12), dma(9), dma(9),
            dma(4), dma(4), dma(2, 6), dma(2, 6), dma(14), dma(14), dma(14), dma(14), dma(7), dma(7),
            dma(3), dma(3), dma(6), dma(6), dma(8), dma(8),
        ],
        compiler_params=pltpu.CompilerParams(
            collective_id=0, has_side_effects=True, vmem_limit_bytes=60 * 1024 * 1024
        ),
    )(t_query, t_key, t_value, out_proj, depth_in, prev_embed, cotangent)
    wide = lambda *shape: jax.ShapeDtypeStruct(shape, F32)
    tokens = pl.BlockSpec((1, 128, 512), lambda i: (0, i, 0))
    weight = pl.BlockSpec((256, 1024), lambda i: (i, 0))
    depth = pl.BlockSpec((64, 256), lambda i: (i, 0))
    specs = [tokens, tokens, tokens, weight, depth]
    dq, dk, dv, dw, dd = pl.pallas_call(
        widen,
        grid=(2,),
        in_specs=specs,
        out_specs=specs,
        out_shape=(wide(1, 256, 512), wide(1, 256, 512), wide(1, 256, 512), wide(512, 1024), wide(HD, 256)),
        compiler_params=pltpu.CompilerParams(vmem_limit_bytes=60 * 1024 * 1024),
    )(dq, dk, dv, dw, dd)
    return dq, dk, dv, dw, jnp.transpose(dd.reshape(2, 64, 256), (0, 2, 1))


def solution(mesh):
    placed = (
        P("grp", "seq", "head"),
        P("grp", "seq", "head"),
        P("grp", "seq", "head"),
        P("head", "seq"),
        P(None, "seq", None),
        P("grp", "head", "seq", None, None),
        P("grp", "head", "seq", None, None),
    )
    return jax.shard_map(
        shards,
        mesh=mesh,
        in_specs=placed,
        out_specs=(
            P("grp", "seq", "head"),
            P("grp", "seq", "head"),
            P("grp", "seq", "head"),
            P("head", "seq"),
            P(None, ("seq", "head"), "grp"),
        ),
        check_vma=False,
    )
```
